128 devices in a mesh: inner: 8 (over z, y_hi), outer: 16 (over x, y_lo, core).
Axes of the slice: x: 4, y: 4 (y_hi: 2, y_lo: 2; y = y_hi * 2 + y_lo), z: 4, core: 2. Of those that a mesh axis runs over, the one named last changes fastest.
Arguments:
- query: float32 [16384, 4096], P(('inner', 'outer')), may hold values from -14 to 14
- keys: float32 [16384, 1024], P(('inner', 'outer')), may hold values from -4.5 to 4.5
- values: float32 [16384, 1024], P(('inner', 'outer')), may hold values from -6 to 6
- grad_out: float32 [16384, 4096], P(('inner', 'outer')), may hold values from -6 to 6
- segment_number: int32 [128, 2], replicated, may hold values from 0 to 255, as said below
Outputs:
- asker_derivative: float32 [16384, 4096], P(('inner', 'outer'))
- grad_keys: float32 [16384, 1024], P(('inner', 'outer'))
- grad_values: float32 [16384, 1024], P(('inner', 'outer'))
The draws below stay inside these ranges and needn't reach their ends.
Inputs may be any that keep to these rules, and one draw needn't show every extreme that they name: `segment_number`: row d holds stretches c and 255 - c with c < 128; every stretch of the sequence appears once.
All inputs are finite; a program needn't handle non-finite values.
Results may differ from the reference program's by a relative error of at most 0.002.
Values sent between devices are 32-bit elements; how exact they have to be, the bound alone decides.
No kernel may reach another device: no remote copies, remote signals or barrier semaphores. Data moves between devices by JAX's collectives and lax.ppermute only.
A program may use at most 128 MiB of HBM per device.

```python
import jax
import jax.numpy as jnp
from jax import lax

ASKER_PLANES = 32
KEY_VALUE_HEADS = 8
HEAD_SIZE = 128
DEVICE_TOKENS = 128
SEQUENCE_TOKENS = 16384
N_INNER = 8
N_OUTER = 16
DEVICES = 128


def draw_query(key, part):
    key = jax.random.fold_in(key, 11)
    base_key = jax.random.fold_in(key, 0)
    array_dims = (DEVICES, DEVICE_TOKENS, KEY_VALUE_HEADS, ASKER_PLANES // KEY_VALUE_HEADS, HEAD_SIZE)
    starting_offset = jnp.clip(jax.random.normal(base_key, array_dims), -4.5, 4.5)
    return starting_offset.reshape(SEQUENCE_TOKENS, ASKER_PLANES * HEAD_SIZE).astype(jnp.float32)


def draw_keys(key, part):
    key = jax.random.fold_in(key, 12)
    array_dims = (DEVICES, DEVICE_TOKENS, KEY_VALUE_HEADS, HEAD_SIZE)
    starting_offset = jnp.clip(jax.random.normal(key, array_dims), -4.5, 4.5)
    return starting_offset.reshape(SEQUENCE_TOKENS, KEY_VALUE_HEADS * HEAD_SIZE).astype(jnp.float32)


def draw_segment_number(key, part):
    key = jax.random.fold_in(key, 13)
    order = jax.random.permutation(key, DEVICES)
    return jnp.stack([order, 2 * DEVICES - 1 - order], axis=1).astype(jnp.int32)


def level_of(own_key, shape, pieces, smallest, top_value):
    factor_of, own = 1.0, jax.random.fold_in(own_key, 6)
    for axis_at, shards_of in pieces:
        steps = jnp.exp(jax.random.uniform(jax.random.fold_in(own, axis_at), (shards_of,), jnp.float32, smallest / len(pieces), top_value / len(pieces)))
        factor_of = factor_of * jnp.repeat(steps, shape[axis_at] // shards_of).reshape([-1 if axis == axis_at else 1 for axis in range(len(shape))])
    return factor_of


def noise(stream_key, shape, width, most, pieces=(), held_as=jnp.bfloat16):
    drawn = jax.random.normal(stream_key, shape, jnp.float32) * width
    if len(pieces) > 0:
        drawn = level_of(stream_key, shape, pieces, -0.22, 0.18) * drawn
    return jnp.clip(drawn, min=-most, max=most).astype(held_as)


def setup_inputs(seed: int = 0) -> dict:
    splits = jax.random.split(jax.random.key(seed), 6)
    query = draw_query(jax.random.fold_in(splits[5], 71), 0)
    keys = draw_keys(jax.random.fold_in(splits[5], 71), 0)
    values = noise(splits[2], (SEQUENCE_TOKENS, KEY_VALUE_HEADS * HEAD_SIZE), 1.0, 6.0, ((0, 128),), jnp.float32)
    grad_out = noise(splits[3], (SEQUENCE_TOKENS, ASKER_PLANES * HEAD_SIZE), 1.0, 6.0, ((0, 128),), jnp.float32)
    segment_number = draw_segment_number(jax.random.fold_in(splits[5], 71), 0)
    return dict(query=query, keys=keys, values=values, grad_out=grad_out, segment_number=segment_number)


def token_positions(segment_number):
    half_rows = DEVICE_TOKENS // 2
    local_rows = jnp.arange(DEVICE_TOKENS, dtype=jnp.int32)
    return segment_number[:, local_rows // half_rows] * half_rows + local_rows % half_rows

def attend(query, keys, values, segment_number):
    positions = token_positions(segment_number)
    group_list = ASKER_PLANES // KEY_VALUE_HEADS
    score_scale = HEAD_SIZE ** (-0.5)
    query_tiles = query.reshape(DEVICES, DEVICE_TOKENS, KEY_VALUE_HEADS, group_list, HEAD_SIZE)
    key_tiles = keys.reshape(DEVICES, DEVICE_TOKENS, KEY_VALUE_HEADS, HEAD_SIZE)
    value_tiles = values.reshape(DEVICES, DEVICE_TOKENS, KEY_VALUE_HEADS, HEAD_SIZE)
    cycle_base = jnp.arange(N_INNER, dtype=jnp.int32) * N_OUTER

    def one_device(device_index):
        outer_index = device_index % N_OUTER
        sender_devices = jnp.concatenate([cycle_base + outer_index, cycle_base + (outer_index - 1) % N_OUTER])
        adjacent_keys = key_tiles[sender_devices].reshape(-1, KEY_VALUE_HEADS, HEAD_SIZE)
        adjacent_values = value_tiles[sender_devices].reshape(-1, KEY_VALUE_HEADS, HEAD_SIZE)
        key_positions = positions[sender_devices].reshape(-1)
        query_here = query_tiles[device_index]
        scores = jnp.einsum('tkgd,lkd->kgtl', query_here, adjacent_keys, precision=lax.Precision.HIGHEST) * score_scale
        visible = key_positions[None, :] <= positions[device_index][:, None]
        scores = jnp.where(visible[None, None], scores, -jnp.inf)
        weights = jax.nn.softmax(scores, axis=-1)
        result = jnp.einsum('kgtl,lkd->tkgd', weights, adjacent_values, precision=lax.Precision.HIGHEST)
        return result.reshape(DEVICE_TOKENS, ASKER_PLANES * HEAD_SIZE)
    output = lax.map(jax.checkpoint(one_device), jnp.arange(DEVICES, dtype=jnp.int32))
    return output.reshape(SEQUENCE_TOKENS, ASKER_PLANES * HEAD_SIZE)

def reference(query, keys, values, grad_out, segment_number):

    def forward(query_in, keys_in, values_in):
        return attend(query_in, keys_in, values_in, segment_number)
    unused, pullback = jax.vjp(forward, query, keys, values)
    asker_derivative, grad_keys, grad_values = pullback(grad_out)
    return (asker_derivative, grad_keys, grad_values)
```

```python
import functools
import math

import jax
import jax.numpy as jnp
from jax import lax
from jax.experimental import pallas as pl
from jax.experimental.pallas import tpu as pltpu
from jax.sharding import PartitionSpec as P

ASKER_PLANES = 32
KEY_VALUE_HEADS = 8
HEAD_SIZE = 128
GROUP_LIST = ASKER_PLANES // KEY_VALUE_HEADS
HEAD_WIDTH = GROUP_LIST * HEAD_SIZE
TILE = 256
SCORE_SCALE = HEAD_SIZE ** (-0.5)
LOG2E = math.log2(math.e)
F32 = jnp.float32
BF16 = jnp.bfloat16


def split2(x):
    high = x.astype(BF16)
    return high, (x - high.astype(F32)).astype(BF16)


def split3(x):
    high = x.astype(BF16)
    rest = x - high.astype(F32)
    middle = rest.astype(BF16)
    return high, middle, (rest - middle.astype(F32)).astype(BF16)


def dot(a, b):
    return jnp.dot(a, b, preferred_element_type=F32)


def fold(x, op):
    return op(x.reshape(x.shape[0] // 8, 8, x.shape[1]), axis=0)


def attention_kernel(
    inner_count, outer_count,
    seg, q_ref, do_ref, own_ref, prev_ref,
    dq_ref, down_ref, dprev_ref,
    rank, low_half, ksort, kcat, vcat, ktrans, dk_acc, dv_acc,
    s_scr, dp_scr,
):
    step = pl.program_id(0)
    blocks = 2 * inner_count
    stretch = own_ref.shape[1] // 2

    @pl.when(step == 0)
    def _():
        outer = lax.axis_index("outer")
        before = lax.rem(outer + outer_count - 1, outer_count)
        first, second = [], []
        for j in range(blocks):
            device = (j % inner_count) * outer_count + (outer if j < inner_count else before)
            first.append(seg[0, device])
            second.append(seg[1, device])
        lows = [jnp.minimum(a, b) for a, b in zip(first, second)]
        for j in range(blocks):
            below = jnp.int32(0)
            for other in range(blocks):
                if other != j:
                    below = below + (lows[other] < lows[j]).astype(jnp.int32)
            rank[j] = below
            low_half[j] = (second[j] < first[j]).astype(jnp.int32)
        for j in range(blocks):
            ref, at = (own_ref, j) if j < inner_count else (prev_ref, j - inner_count)
            for half in range(2):
                slot = jnp.where(low_half[j] == half, rank[j], 2 * blocks - 1 - rank[j])
                to = pl.ds(pl.multiple_of(slot * stretch, stretch), stretch)
                both = ref[at, half * stretch : (half + 1) * stretch, :]
                key, value = both[:, :HEAD_SIZE], both[:, HEAD_SIZE:]
                ksort[to, :] = key
                h, m, l = split3(key)
                kcat[to, :] = jnp.concatenate([h, h, m, h, l, m], axis=1)
                h, l = split2(value)
                vcat[to, :] = jnp.concatenate([h, h, l, l], axis=1)
        for t in range(ksort.shape[0] // TILE):
            h, l = split2(ksort[t * TILE : (t + 1) * TILE, :].T)
            ktrans[t] = jnp.concatenate([h, l], axis=0)
        dk_acc[...] = jnp.zeros_like(dk_acc)
        dv_acc[...] = jnp.zeros_like(dv_acc)

    place = rank[step]
    low = low_half[step]
    per_tile = TILE // stretch
    for kind in range(2):
        offset = pl.multiple_of(jnp.where(low == kind, 0, stretch), stretch)
        reach = place if kind == 0 else 2 * blocks - 1 - place
        last = reach // per_tile
        rows = pl.ds(offset, stretch)
        q = jnp.concatenate(
            [q_ref[0, rows, g * HEAD_SIZE : (g + 1) * HEAD_SIZE] for g in range(GROUP_LIST)], axis=0
        ) * (SCORE_SCALE * LOG2E)
        do = jnp.concatenate(
            [do_ref[0, rows, g * HEAD_SIZE : (g + 1) * HEAD_SIZE] for g in range(GROUP_LIST)], axis=0
        )
        h, m, l = split3(q.T)
        qt = jnp.concatenate([h, m, h, l, h, m], axis=0)
        h, l = split2(q)
        q_pair = jnp.concatenate([h, l], axis=1)
        q_rhs = jnp.concatenate([q_pair, q_pair], axis=0)
        h, l = split2(do.T)
        dot_t = jnp.concatenate([h, l, h, l], axis=0)
        h, l = split2(do)
        do_pair = jnp.concatenate([h, l], axis=1)
        do_rhs = jnp.concatenate([do_pair, do_pair], axis=0)

        def scores(t):
            at = pl.ds(pl.multiple_of(t * TILE, TILE), TILE)
            return at, dot(kcat[at, :], qt), dot(vcat[at, :], dot_t)

        def open_tile(t, peak):
            at, s, dp = scores(t)
            s_scr[at, :] = s
            dp_scr[at, :] = dp
            return jnp.maximum(peak, fold(s, jnp.max))

        peak = lax.fori_loop(0, last, open_tile, jnp.full((8, TILE), -jnp.inf, F32))
        at, s, dp = scores(last)
        key_at = last * TILE + lax.broadcasted_iota(jnp.int32, (TILE, TILE), 0)
        token = lax.rem(lax.broadcasted_iota(jnp.int32, (TILE, TILE), 1), stretch)
        s = jnp.where(key_at <= reach * stretch + token, s, -jnp.inf)
        s_scr[at, :] = s
        dp_scr[at, :] = dp
        peak = jnp.max(jnp.maximum(peak, fold(s, jnp.max)), axis=0, keepdims=True)

        def sums(t, carry):
            total, delta = carry
            at = pl.ds(pl.multiple_of(t * TILE, TILE), TILE)
            e = jnp.exp2(s_scr[at, :] - peak)
            s_scr[at, :] = e
            return total + fold(e, jnp.sum), delta + fold(e * dp_scr[at, :], jnp.sum)

        zero = jnp.zeros((8, TILE), F32)
        total, delta = lax.fori_loop(0, last + 1, sums, (zero, zero))
        inverse = 1.0 / jnp.sum(total, axis=0, keepdims=True)
        delta = jnp.sum(delta, axis=0, keepdims=True) * inverse

        def grads(t, dqt):
            at = pl.ds(pl.multiple_of(t * TILE, TILE), TILE)
            p = s_scr[at, :] * inverse
            ds = p * (dp_scr[at, :] - delta)
            dv_acc[at, :] += dot(jnp.concatenate(split2(p), axis=1), do_rhs)
            h, l = split2(ds)
            dk_acc[at, :] += dot(jnp.concatenate([h, l], axis=1), q_rhs)
            return dqt + dot(ktrans[t], h) + dot(ktrans[t], l)

        dqt = lax.fori_loop(0, last + 1, grads, jnp.zeros((2 * HEAD_SIZE, TILE), F32))
        dq = ((dqt[:HEAD_SIZE] + dqt[HEAD_SIZE:]) * SCORE_SCALE).T
        for g in range(GROUP_LIST):
            dq_ref[0, rows, g * HEAD_SIZE : (g + 1) * HEAD_SIZE] = dq[g * stretch : (g + 1) * stretch]

    @pl.when(step == pl.num_programs(0) - 1)
    def _():
        for j in range(blocks):
            ref, at = (down_ref, j) if j < inner_count else (dprev_ref, j - inner_count)
            for half in range(2):
                slot = jnp.where(low_half[j] == half, rank[j], 2 * blocks - 1 - rank[j])
                came = pl.ds(pl.multiple_of(slot * stretch, stretch), stretch)
                to = slice(half * stretch, (half + 1) * stretch)
                dk, dv = dk_acc[came, :], dv_acc[came, :]
                ref[at, to, :HEAD_SIZE] = (dk[:, :HEAD_SIZE] + dk[:, HEAD_SIZE:]) * (1.0 / LOG2E)
                ref[at, to, HEAD_SIZE:] = dv[:, :HEAD_SIZE] + dv[:, HEAD_SIZE:]


def attention(inner_count, outer_count, seg, q, do, own, prev):
    rows = own.shape[1]
    keys = 2 * inner_count * rows
    block = lambda width: pl.BlockSpec((1, rows, width), lambda i: (i, 0, 0))
    whole = pl.BlockSpec((inner_count, rows, 2 * HEAD_SIZE), lambda i: (0, 0, 0))
    kv_shape = jax.ShapeDtypeStruct(own.shape, F32)
    return pl.pallas_call(
        functools.partial(attention_kernel, inner_count, outer_count),
        grid=(inner_count,),
        in_specs=[
            pl.BlockSpec(memory_space=pltpu.SMEM),
            block(HEAD_WIDTH), block(HEAD_WIDTH), whole, whole,
        ],
        out_specs=[block(HEAD_WIDTH), whole, whole],
        out_shape=[jax.ShapeDtypeStruct((inner_count, rows, HEAD_WIDTH), F32), kv_shape, kv_shape],
        scratch_shapes=[
            pltpu.SMEM((2 * inner_count,), jnp.int32),
            pltpu.SMEM((2 * inner_count,), jnp.int32),
            pltpu.VMEM((keys, HEAD_SIZE), F32),
            pltpu.VMEM((keys, 6 * HEAD_SIZE), BF16),
            pltpu.VMEM((keys, 4 * HEAD_SIZE), BF16),
            pltpu.VMEM((keys // TILE, 2 * HEAD_SIZE, TILE), BF16),
            pltpu.VMEM((keys, 2 * HEAD_SIZE), F32),
            pltpu.VMEM((keys, 2 * HEAD_SIZE), F32),
            pltpu.VMEM((keys, TILE), F32),
            pltpu.VMEM((keys, TILE), F32),
        ],
        compiler_params=pltpu.CompilerParams(vmem_limit_bytes=48 * 1024 * 1024),
        name="attention",
    )(seg, q, do, own, prev)


def from_behind(x, axis, by):
    size = lax.axis_size(axis)
    return lax.ppermute(x, axis, [(i, (i + by) % size) for i in range(size)])


def by_head(x, heads):
    rows = x.shape[0]
    return x.reshape(rows, heads, -1).transpose(1, 0, 2)


def local(query, keys, values, grad_out, segment_number):
    inner_count = lax.axis_size("inner")
    outer_count = lax.axis_size("outer")
    rows = query.shape[0]
    swap = lambda x: lax.all_to_all(x, "inner", 0, 0)
    own = swap(jnp.concatenate([by_head(keys, inner_count), by_head(values, inner_count)], axis=2))
    prev = from_behind(own, "outer", 1)
    both = swap(jnp.stack([by_head(query, inner_count), by_head(grad_out, inner_count)], axis=1))
    q, do = both[:, 0], both[:, 1]
    dq, down, dprev = attention(inner_count, outer_count, segment_number.T, q, do, own, prev)
    back = from_behind(dprev, "outer", -1)
    dq = swap(dq).transpose(1, 0, 2).reshape(rows, -1)
    dkv = swap(down + back).transpose(1, 0, 2)
    return (
        dq,
        dkv[:, :, :HEAD_SIZE].reshape(rows, -1),
        dkv[:, :, HEAD_SIZE:].reshape(rows, -1),
    )


def solution(mesh):
    spec = P(("inner", "outer"), None)
    return jax.shard_map(
        local,
        mesh=mesh,
        in_specs=(spec, spec, spec, spec, P()),
        out_specs=(spec, spec, spec),
        check_vma=False,
    )
```

```python
import functools
import math

import jax
import jax.numpy as jnp
from jax import lax
from jax.experimental import pallas as pl
from jax.experimental.pallas import tpu as pltpu
from jax.sharding import PartitionSpec as P

ASKER_PLANES = 32
KEY_VALUE_HEADS = 8
HEAD_SIZE = 128
GROUP_LIST = ASKER_PLANES // KEY_VALUE_HEADS
HEAD_WIDTH = GROUP_LIST * HEAD_SIZE
TILE = 256
SCORE_SCALE = HEAD_SIZE ** (-0.5)
LOG2E = math.log2(math.e)
F32 = jnp.float32
BF16 = jnp.bfloat16
SMEM = pl.BlockSpec(memory_space=pltpu.SMEM)


def split2(x):
    high = x.astype(BF16)
    return high, (x - high.astype(F32)).astype(BF16)


def split3(x):
    high = x.astype(BF16)
    rest = x - high.astype(F32)
    middle = rest.astype(BF16)
    return high, middle, (rest - middle.astype(F32)).astype(BF16)


def dot(a, b):
    return jnp.dot(a, b, preferred_element_type=F32)


def fold(x, op):
    return op(x.reshape(x.shape[0] // 8, 8, x.shape[1]), axis=0)


def aligned(start, size):
    return pl.ds(pl.multiple_of(start, size), size)


def attention_kernel(inner_count, outer_count, is_high, seg, q_ref, own_ref, prev_ref, *refs):
    if is_high:
        dq_ref, down_high, dprev_high, down_low, dprev_low, *refs = refs
    else:
        down_in, dprev_in, dq_ref, down_low, dprev_low, *refs = refs
    rank, ksort, kcat, vcat, ktrans, dk_acc, dv_acc, s_scr, dp_scr = refs
    step = pl.program_id(0)
    blocks = 2 * inner_count
    stretch = q_ref.shape[2]
    per_tile = TILE // stretch

    def slots():
        for j in range(blocks):
            yield j, 0, rank[j]
            if is_high:
                yield j, 1, 2 * blocks - 1 - rank[j]

    @pl.when(step == 0)
    def _():
        outer = lax.axis_index("outer")
        before = lax.rem(outer + outer_count - 1, outer_count)
        lows = []
        for j in range(blocks):
            device = (j % inner_count) * outer_count + (outer if j < inner_count else before)
            lows.append(jnp.minimum(seg[0, device], seg[1, device]))
        for j in range(blocks):
            below = jnp.int32(0)
            for other in range(blocks):
                if other != j:
                    below = below + (lows[other] < lows[j]).astype(jnp.int32)
            rank[j] = below
        for j, half, slot in slots():
            ref, at = (own_ref, j) if j < inner_count else (prev_ref, j - inner_count)
            to = aligned(slot * stretch, stretch)
            both = ref[at, half * stretch : (half + 1) * stretch, :]
            key, value = both[:, :HEAD_SIZE], both[:, HEAD_SIZE:]
            ksort[to, :] = key
            h, m, l = split3(key)
            kcat[to, :] = jnp.concatenate([h, h, m, h, l, m], axis=1)
            h, l = split2(value)
            vcat[to, :] = jnp.concatenate([h, h, l, l], axis=1)
        for t in range(ksort.shape[0] // TILE):
            h, l = split2(ksort[t * TILE : (t + 1) * TILE, :].T)
            ktrans[t] = jnp.concatenate([h, l], axis=0)
        dk_acc[...] = jnp.zeros_like(dk_acc)
        dv_acc[...] = jnp.zeros_like(dv_acc)

    reach = 2 * blocks - 1 - rank[step] if is_high else rank[step]
    last = reach // per_tile
    heads = [slice(g * HEAD_SIZE, (g + 1) * HEAD_SIZE) for g in range(GROUP_LIST)]
    q = jnp.concatenate([q_ref[0, 0, :, g] for g in heads], axis=0) * (SCORE_SCALE * LOG2E)
    do = jnp.concatenate([q_ref[0, 1, :, g] for g in heads], axis=0)
    h, m, l = split3(q.T)
    qt = jnp.concatenate([h, m, h, l, h, m], axis=0)
    h, l = split2(q)
    q_pair = jnp.concatenate([h, l], axis=1)
    q_rhs = jnp.concatenate([q_pair, q_pair], axis=0)
    h, l = split2(do.T)
    dot_t = jnp.concatenate([h, l, h, l], axis=0)
    h, l = split2(do)
    do_pair = jnp.concatenate([h, l], axis=1)
    do_rhs = jnp.concatenate([do_pair, do_pair], axis=0)

    def scores(t):
        at = aligned(t * TILE, TILE)
        return at, dot(kcat[at, :], qt), dot(vcat[at, :], dot_t)

    def open_tile(t, peak):
        at, s, dp = scores(t)
        s_scr[at, :] = s
        dp_scr[at, :] = dp
        return jnp.maximum(peak, fold(s, jnp.max))

    peak = lax.fori_loop(0, last, open_tile, jnp.full((8, TILE), -jnp.inf, F32))
    at, s, dp = scores(last)
    key_at = last * TILE + lax.broadcasted_iota(jnp.int32, (TILE, TILE), 0)
    token = lax.rem(lax.broadcasted_iota(jnp.int32, (TILE, TILE), 1), stretch)
    s = jnp.where(key_at <= reach * stretch + token, s, -jnp.inf)
    s_scr[at, :] = s
    dp_scr[at, :] = dp
    peak = jnp.max(jnp.maximum(peak, fold(s, jnp.max)), axis=0, keepdims=True)

    def sums(t, carry):
        total, delta = carry
        at = aligned(t * TILE, TILE)
        e = jnp.exp2(s_scr[at, :] - peak)
        s_scr[at, :] = e
        return total + fold(e, jnp.sum), delta + fold(e * dp_scr[at, :], jnp.sum)

    zero = jnp.zeros((8, TILE), F32)
    total, delta = lax.fori_loop(0, last + 1, sums, (zero, zero))
    inverse = 1.0 / jnp.sum(total, axis=0, keepdims=True)
    delta = jnp.sum(delta, axis=0, keepdims=True) * inverse

    def grads(t, dqt):
        at = aligned(t * TILE, TILE)
        p = s_scr[at, :] * inverse
        ds = p * (dp_scr[at, :] - delta)
        dv_acc[at, :] += dot(jnp.concatenate(split2(p), axis=1), do_rhs)
        h, l = split2(ds)
        dk_acc[at, :] += dot(jnp.concatenate([h, l], axis=1), q_rhs)
        return dqt + dot(ktrans[t], h) + dot(ktrans[t], l)

    dqt = lax.fori_loop(0, last + 1, grads, jnp.zeros((2 * HEAD_SIZE, TILE), F32))
    dq = ((dqt[:HEAD_SIZE] + dqt[HEAD_SIZE:]) * SCORE_SCALE).T
    for i, g in enumerate(heads):
        dq_ref[0, :, g] = dq[i * stretch : (i + 1) * stretch]

    @pl.when(step == pl.num_programs(0) - 1)
    def _():
        for j, half, slot in slots():
            came = aligned(slot * stretch, stretch)
            dk, dv = dk_acc[came, :], dv_acc[came, :]
            dk = (dk[:, :HEAD_SIZE] + dk[:, HEAD_SIZE:]) * (1.0 / LOG2E)
            dv = dv[:, :HEAD_SIZE] + dv[:, HEAD_SIZE:]
            is_own = j < inner_count
            at = j if is_own else j - inner_count
            if half == 1:
                ref = down_high if is_own else dprev_high
            else:
                ref = down_low if is_own else dprev_low
                if not is_high:
                    earlier = down_in if is_own else dprev_in
                    dk = dk + earlier[at, :, :HEAD_SIZE]
                    dv = dv + earlier[at, :, HEAD_SIZE:]
            ref[at, :, :HEAD_SIZE] = dk
            ref[at, :, HEAD_SIZE:] = dv


def attention(is_high, outer_count, seg, q, own, prev, *earlier):
    inner_count, rows, _ = own.shape
    stretch = rows // 2
    key_rows = rows if is_high else stretch
    keys = 2 * inner_count * key_rows
    whole = lambda r: pl.BlockSpec((inner_count, r, 2 * HEAD_SIZE), lambda i: (0, 0, 0))
    half_kv = jax.ShapeDtypeStruct((inner_count, stretch, 2 * HEAD_SIZE), F32)
    kv_outs = 4 if is_high else 2
    tiles = 52 if is_high else 20
    return pl.pallas_call(
        functools.partial(attention_kernel, inner_count, outer_count, is_high),
        grid=(inner_count,),
        in_specs=[
            SMEM,
            pl.BlockSpec((1, 2, stretch, HEAD_WIDTH), lambda i: (i, 0, 0, 0)),
            whole(key_rows), whole(key_rows),
        ] + [whole(stretch)] * len(earlier),
        out_specs=[pl.BlockSpec((1, stretch, HEAD_WIDTH), lambda i: (i, 0, 0))] + [whole(stretch)] * kv_outs,
        out_shape=[jax.ShapeDtypeStruct((inner_count, stretch, HEAD_WIDTH), F32)] + [half_kv] * kv_outs,
        scratch_shapes=[
            pltpu.SMEM((2 * inner_count,), jnp.int32),
            pltpu.VMEM((keys, HEAD_SIZE), F32),
            pltpu.VMEM((keys, 6 * HEAD_SIZE), BF16),
            pltpu.VMEM((keys, 4 * HEAD_SIZE), BF16),
            pltpu.VMEM((keys // TILE, 2 * HEAD_SIZE, TILE), BF16),
            pltpu.VMEM((keys, 2 * HEAD_SIZE), F32),
            pltpu.VMEM((keys, 2 * HEAD_SIZE), F32),
            pltpu.VMEM((keys, TILE), F32),
            pltpu.VMEM((keys, TILE), F32),
        ],
        cost_estimate=pl.CostEstimate(
            flops=tiles * 1_000_000_000, bytes_accessed=8 << 20, transcendentals=0
        ),
        compiler_params=pltpu.CompilerParams(vmem_limit_bytes=40 * 1024 * 1024),
        name="attention_high" if is_high else "attention_low",
    )(seg, q, own, prev, *earlier)


def low_first(seg, outer_count, stretch):
    device = lax.axis_index("inner") * outer_count + lax.axis_index("outer")
    low = jnp.where(seg[0, device] < seg[1, device], 0, stretch)
    return aligned(low, stretch), aligned(stretch - low, stretch)


def pack_kv_kernel(outer_count, seg, k_ref, v_ref, out_ref):
    stretch = k_ref.shape[0] // 2
    for i, rows in enumerate(low_first(seg, outer_count, stretch)):
        at = slice(i * stretch, (i + 1) * stretch)
        for h in range(out_ref.shape[0]):
            columns = slice(h * HEAD_SIZE, (h + 1) * HEAD_SIZE)
            out_ref[h, at, :HEAD_SIZE] = k_ref[rows, columns]
            out_ref[h, at, HEAD_SIZE:] = v_ref[rows, columns]


def pack_kv(outer_count, seg, keys, values, heads):
    rows, width = keys.shape
    whole = pl.BlockSpec((rows, width), lambda: (0, 0))
    shape = (heads, rows, 2 * HEAD_SIZE)
    return pl.pallas_call(
        functools.partial(pack_kv_kernel, outer_count),
        in_specs=[SMEM, whole, whole],
        out_specs=pl.BlockSpec(shape, lambda: (0, 0, 0)),
        out_shape=jax.ShapeDtypeStruct(shape, F32),
        name="pack_kv",
    )(seg, keys, values)


def pack_q_kernel(outer_count, seg, q_ref, do_ref, low_ref, high_ref):
    stretch = q_ref.shape[0] // 2
    low, high = low_first(seg, outer_count, stretch)
    low_ref[0, 0], low_ref[0, 1] = q_ref[low, :], do_ref[low, :]
    high_ref[0, 0], high_ref[0, 1] = q_ref[high, :], do_ref[high, :]


def pack_q(outer_count, seg, query, grad_out, heads):
    rows = query.shape[0]
    shape = (2, rows // 2, HEAD_WIDTH)
    half = pl.BlockSpec((1, *shape), lambda h: (h, 0, 0, 0))
    return pl.pallas_call(
        functools.partial(pack_q_kernel, outer_count),
        grid=(heads,),
        in_specs=[SMEM] + [pl.BlockSpec((rows, HEAD_WIDTH), lambda h: (0, h))] * 2,
        out_specs=[half, half],
        out_shape=[jax.ShapeDtypeStruct((heads, *shape), F32)] * 2,
        name="pack_q",
    )(seg, query, grad_out)


def unpack_q_kernel(outer_count, seg, low_ref, high_ref, out_ref):
    low, high = low_first(seg, outer_count, low_ref.shape[1])
    out_ref[low, :] = low_ref[0]
    out_ref[high, :] = high_ref[0]


def unpack_q(outer_count, seg, low, high):
    heads, stretch, width = low.shape
    half = pl.BlockSpec((1, stretch, width), lambda h: (h, 0, 0))
    return pl.pallas_call(
        functools.partial(unpack_q_kernel, outer_count),
        grid=(heads,),
        in_specs=[SMEM, half, half],
        out_specs=pl.BlockSpec((2 * stretch, width), lambda h: (0, h)),
        out_shape=jax.ShapeDtypeStruct((2 * stretch, heads * width), F32),
        name="unpack_q",
    )(seg, low, high)


def unpack_kv_kernel(outer_count, seg, low_ref, high_ref, k_ref, v_ref):
    for ref, rows in zip((low_ref, high_ref), low_first(seg, outer_count, low_ref.shape[1])):
        for h in range(ref.shape[0]):
            columns = slice(h * HEAD_SIZE, (h + 1) * HEAD_SIZE)
            k_ref[rows, columns] = ref[h, :, :HEAD_SIZE]
            v_ref[rows, columns] = ref[h, :, HEAD_SIZE:]


def unpack_kv(outer_count, seg, low, high):
    heads, stretch, _ = low.shape
    whole = pl.BlockSpec(low.shape, lambda: (0, 0, 0))
    shape = (2 * stretch, heads * HEAD_SIZE)
    return pl.pallas_call(
        functools.partial(unpack_kv_kernel, outer_count),
        in_specs=[SMEM, whole, whole],
        out_specs=[pl.BlockSpec(shape, lambda: (0, 0))] * 2,
        out_shape=[jax.ShapeDtypeStruct(shape, F32)] * 2,
        name="unpack_kv",
    )(seg, low, high)


def from_behind(x, axis, by):
    size = lax.axis_size(axis)
    return lax.ppermute(x, axis, [(i, (i + by) % size) for i in range(size)])


def local(query, keys, values, grad_out, segment_number):
    inner_count = lax.axis_size("inner")
    outer_count = lax.axis_size("outer")
    swap = lambda x: lax.all_to_all(x, "inner", 0, 0)
    seg = segment_number.T
    own = swap(pack_kv(outer_count, seg, keys, values, inner_count))
    q_low, q_high = pack_q(outer_count, seg, query, grad_out, inner_count)
    prev = from_behind(own, "outer", 1)
    q_high = swap(q_high)
    q_low = swap(q_low)
    dq_high, down_high, dprev_high, down_low, dprev_low = attention(
        True, outer_count, seg, q_high, own, prev
    )
    back_high = from_behind(dprev_high, "outer", -1)
    dq_high = swap(dq_high)
    dq_low, down_low, dprev_low = attention(
        False, outer_count, seg, q_low, own, prev, down_low, dprev_low
    )
    dkv_high = swap(down_high + back_high)
    back_low = from_behind(dprev_low, "outer", -1)
    dq_low = swap(dq_low)
    dkv_low = swap(down_low + back_low)
    grad_query = unpack_q(outer_count, seg, dq_low, dq_high)
    grad_keys, grad_values = unpack_kv(outer_count, seg, dkv_low, dkv_high)
    return grad_query, grad_keys, grad_values


def solution(mesh):
    spec = P(("inner", "outer"), None)
    return jax.shard_map(
        local,
        mesh=mesh,
        in_specs=(spec, spec, spec, spec, P()),
        out_specs=(spec, spec, spec),
        check_vma=False,
    )
```

```python
import functools
import math

import jax
import jax.numpy as jnp
from jax import lax
from jax.experimental import pallas as pl
from jax.experimental.pallas import tpu as pltpu
from jax.sharding import PartitionSpec as P

ASKER_PLANES = 32
KEY_VALUE_HEADS = 8
HEAD_SIZE = 128
GROUP_LIST = ASKER_PLANES // KEY_VALUE_HEADS
HEAD_WIDTH = GROUP_LIST * HEAD_SIZE
TILE = 256
KEY_TILE = 256
SCORE_SCALE = HEAD_SIZE ** (-0.5)
LOG2E = math.log2(math.e)
F32 = jnp.float32
BF16 = jnp.bfloat16
SMEM = pl.BlockSpec(memory_space=pltpu.SMEM)


def split2(x):
    high = x.astype(BF16)
    return high, (x - high.astype(F32)).astype(BF16)


def split3(x):
    high = x.astype(BF16)
    rest = x - high.astype(F32)
    middle = rest.astype(BF16)
    return high, middle, (rest - middle.astype(F32)).astype(BF16)


def dot(a, b):
    return jnp.dot(a, b, preferred_element_type=F32)


def fold(x, op):
    return op(x.reshape(x.shape[0] // 8, 8, x.shape[1]), axis=0)


def aligned(start, size):
    return pl.ds(pl.multiple_of(start, size), size)


def attention_kernel(inner_count, outer_count, is_high, seg, q_ref, own_ref, prev_ref, *refs):
    if is_high:
        dq_ref, down_ref, dprev_ref, *refs = refs
    else:
        down_in, dprev_in, dq_ref, down_ref, dprev_ref, *refs = refs
    rank, ksort, kcat, vcat, ktrans, dk_acc, dv_acc, s_scr, dp_scr, peaks = refs
    step = pl.program_id(0)
    blocks = 2 * inner_count
    stretch = q_ref.shape[2]
    per_tile = KEY_TILE // stretch

    def slots():
        for j in range(blocks):
            yield j, 0, rank[j]
            if is_high:
                yield j, 1, 2 * blocks - 1 - rank[j]

    @pl.when(step == 0)
    def _():
        outer = lax.axis_index("outer")
        before = lax.rem(outer + outer_count - 1, outer_count)
        lows = []
        for j in range(blocks):
            device = (j % inner_count) * outer_count + (outer if j < inner_count else before)
            lows.append(jnp.minimum(seg[0, device], seg[1, device]))
        for j in range(blocks):
            below = jnp.int32(0)
            for other in range(blocks):
                if other != j:
                    below = below + (lows[other] < lows[j]).astype(jnp.int32)
            rank[j] = below
        for j, half, slot in slots():
            ref, at = (own_ref, j) if j < inner_count else (prev_ref, j - inner_count)
            to = aligned(slot * stretch, stretch)
            both = ref[at, half * stretch : (half + 1) * stretch, :]
            key, value = both[:, :HEAD_SIZE], both[:, HEAD_SIZE:]
            ksort[to, :] = key
            h, m, l = split3(key)
            kcat[to, :] = jnp.concatenate([h, h, m, h, l, m], axis=1)
            h, l = split2(value)
            vcat[to, :] = jnp.concatenate([h, h, l, l], axis=1)
        for t in range(ksort.shape[0] // KEY_TILE):
            h, l = split2(ksort[t * KEY_TILE : (t + 1) * KEY_TILE, :].T)
            ktrans[t] = jnp.concatenate([h, l], axis=0)
        dk_acc[...] = jnp.zeros_like(dk_acc)
        dv_acc[...] = jnp.zeros_like(dv_acc)

    reach = 2 * blocks - 1 - rank[step] if is_high else rank[step]
    last = reach // per_tile
    heads = [slice(g * HEAD_SIZE, (g + 1) * HEAD_SIZE) for g in range(GROUP_LIST)]
    q = jnp.concatenate([q_ref[0, 0, :, g] for g in heads], axis=0) * (SCORE_SCALE * LOG2E)
    do = jnp.concatenate([q_ref[0, 1, :, g] for g in heads], axis=0)
    h, m, l = split3(q.T)
    qt = jnp.concatenate([h, m, h, l, h, m], axis=0)
    h, l = split2(q)
    q_pair = jnp.concatenate([h, l], axis=1)
    q_rhs = jnp.concatenate([q_pair, q_pair], axis=0)
    h, l = split2(do.T)
    dot_t = jnp.concatenate([h, l, h, l], axis=0)
    h, l = split2(do)
    do_pair = jnp.concatenate([h, l], axis=1)
    do_rhs = jnp.concatenate([do_pair, do_pair], axis=0)

    def open_tile(t, carry, visible=None):
        peak, total, delta = carry
        at = slice(t * KEY_TILE, (t + 1) * KEY_TILE)
        s = dot(kcat[at, :], qt)
        dp = dot(vcat[at, :], dot_t)
        if visible is not None:
            s = jnp.where(visible, s, -jnp.inf)
        higher = jnp.maximum(peak, jnp.max(s, axis=0, keepdims=True))
        e = jnp.exp2(s - higher)
        s_scr[at, :] = e
        dp_scr[at, :] = dp
        peaks[t] = higher
        shrink = jnp.exp2(peak - higher)
        total = total * shrink + jnp.sum(e, axis=0, keepdims=True)
        delta = delta * shrink + jnp.sum(e * dp, axis=0, keepdims=True)
        return higher, total, delta

    key_at = lax.broadcasted_iota(jnp.int32, (KEY_TILE, TILE), 0)
    token = lax.rem(lax.broadcasted_iota(jnp.int32, (KEY_TILE, TILE), 1), stretch)

    def whole(count):
        carry = (jnp.full((1, TILE), -jnp.inf, F32), *[jnp.zeros((1, TILE), F32)] * 2)
        for t in range(count):
            visible = None
            if t == count - 1:
                visible = key_at <= (reach - t * per_tile) * stretch + token
            carry = open_tile(t, carry, visible)
        peak, total, delta = carry
        inverse = 1.0 / total
        delta = delta * inverse
        dqt = dqt_low = None
        for t in range(count):
            at = slice(t * KEY_TILE, (t + 1) * KEY_TILE)
            p = s_scr[at, :] * (jnp.exp2(peaks[t] - peak) * inverse)
            ds = p * (dp_scr[at, :] - delta)
            dv_acc[at, :] += dot(jnp.concatenate(split2(p), axis=1), do_rhs)
            h, l = split2(ds)
            dk_acc[at, :] += dot(jnp.concatenate([h, l], axis=1), q_rhs)
            term = dot(ktrans[t], h)
            low_term = dot(ktrans[t, :HEAD_SIZE], l)
            dqt = term if dqt is None else dqt + term
            dqt_low = low_term if dqt_low is None else dqt_low + low_term
        dq = ((dqt[:HEAD_SIZE] + dqt[HEAD_SIZE:] + dqt_low) * SCORE_SCALE).T
        for i, g in enumerate(heads):
            dq_ref[0, :, g] = dq[i * stretch : (i + 1) * stretch]

    tiles = blocks // per_tile
    for count in range(tiles + 1, 2 * tiles + 1) if is_high else range(1, tiles + 1):
        pl.when(last == count - 1)(functools.partial(whole, count))

    @pl.when(step == pl.num_programs(0) - 1)
    def _():
        for j, half, slot in slots():
            came = aligned(slot * stretch, stretch)
            dk, dv = dk_acc[came, :], dv_acc[came, :]
            dk = (dk[:, :HEAD_SIZE] + dk[:, HEAD_SIZE:]) * (1.0 / LOG2E)
            dv = dv[:, :HEAD_SIZE] + dv[:, HEAD_SIZE:]
            is_own = j < inner_count
            at = j if is_own else j - inner_count
            ref = down_ref if is_own else dprev_ref
            rows = slice(half * stretch, (half + 1) * stretch)
            if not is_high:
                earlier = down_in if is_own else dprev_in
                dk = dk + earlier[at, rows, :HEAD_SIZE]
                dv = dv + earlier[at, rows, HEAD_SIZE:]
                ref[at, stretch:, :] = earlier[at, stretch:, :]
            ref[at, rows, :HEAD_SIZE] = dk
            ref[at, rows, HEAD_SIZE:] = dv


def attention(is_high, outer_count, seg, q, own, prev, *earlier):
    inner_count, rows, _ = own.shape
    stretch = rows // 2
    key_rows = rows if is_high else stretch
    keys = 2 * inner_count * key_rows
    whole = lambda r: pl.BlockSpec((inner_count, r, 2 * HEAD_SIZE), lambda i: (0, 0, 0))
    tiles = 52 if is_high else 20
    return pl.pallas_call(
        functools.partial(attention_kernel, inner_count, outer_count, is_high),
        grid=(inner_count,),
        in_specs=[
            SMEM,
            pl.BlockSpec((1, 2, stretch, HEAD_WIDTH), lambda i: (i, 0, 0, 0)),
            whole(key_rows), whole(key_rows),
        ] + [whole(rows)] * len(earlier),
        out_specs=[pl.BlockSpec((1, stretch, HEAD_WIDTH), lambda i: (i, 0, 0))] + [whole(rows)] * 2,
        out_shape=[jax.ShapeDtypeStruct((inner_count, stretch, HEAD_WIDTH), F32)] + [jax.ShapeDtypeStruct(own.shape, F32)] * 2,
        scratch_shapes=[
            pltpu.SMEM((2 * inner_count,), jnp.int32),
            pltpu.VMEM((keys, HEAD_SIZE), F32),
            pltpu.VMEM((keys, 6 * HEAD_SIZE), BF16),
            pltpu.VMEM((keys, 4 * HEAD_SIZE), BF16),
            pltpu.VMEM((keys // KEY_TILE, 2 * HEAD_SIZE, KEY_TILE), BF16),
            pltpu.VMEM((keys, 2 * HEAD_SIZE), F32),
            pltpu.VMEM((keys, 2 * HEAD_SIZE), F32),
            pltpu.VMEM((keys, TILE), F32),
            pltpu.VMEM((keys, TILE), F32),
            pltpu.VMEM((keys // KEY_TILE, 1, TILE), F32),
        ],
        cost_estimate=pl.CostEstimate(
            flops=tiles * 1_000_000_000, bytes_accessed=8 << 20, transcendentals=0
        ),
        compiler_params=pltpu.CompilerParams(vmem_limit_bytes=40 * 1024 * 1024),
        name="attention_high" if is_high else "attention_low",
    )(seg, q, own, prev, *earlier)


def low_first(seg, outer_count, stretch):
    device = lax.axis_index("inner") * outer_count + lax.axis_index("outer")
    low = jnp.where(seg[0, device] < seg[1, device], 0, stretch)
    return aligned(low, stretch), aligned(stretch - low, stretch)


def pack_kv_kernel(outer_count, seg, k_ref, v_ref, out_ref):
    stretch = k_ref.shape[0] // 2
    for i, rows in enumerate(low_first(seg, outer_count, stretch)):
        at = slice(i * stretch, (i + 1) * stretch)
        for h in range(out_ref.shape[0]):
            columns = slice(h * HEAD_SIZE, (h + 1) * HEAD_SIZE)
            out_ref[h, at, :HEAD_SIZE] = k_ref[rows, columns]
            out_ref[h, at, HEAD_SIZE:] = v_ref[rows, columns]


def pack_kv(outer_count, seg, keys, values, heads):
    rows, width = keys.shape
    whole = pl.BlockSpec((rows, width), lambda: (0, 0))
    shape = (heads, rows, 2 * HEAD_SIZE)
    return pl.pallas_call(
        functools.partial(pack_kv_kernel, outer_count),
        in_specs=[SMEM, whole, whole],
        out_specs=pl.BlockSpec(shape, lambda: (0, 0, 0)),
        out_shape=jax.ShapeDtypeStruct(shape, F32),
        name="pack_kv",
    )(seg, keys, values)


def pack_q_kernel(outer_count, seg, q_ref, do_ref, low_ref, high_ref):
    stretch = q_ref.shape[0] // 2
    low, high = low_first(seg, outer_count, stretch)
    low_ref[0, 0], low_ref[0, 1] = q_ref[low, :], do_ref[low, :]
    high_ref[0, 0], high_ref[0, 1] = q_ref[high, :], do_ref[high, :]


def pack_q(outer_count, seg, query, grad_out, heads):
    rows = query.shape[0]
    shape = (2, rows // 2, HEAD_WIDTH)
    half = pl.BlockSpec((1, *shape), lambda h: (h, 0, 0, 0))
    return pl.pallas_call(
        functools.partial(pack_q_kernel, outer_count),
        grid=(heads,),
        in_specs=[SMEM] + [pl.BlockSpec((rows, HEAD_WIDTH), lambda h: (0, h))] * 2,
        out_specs=[half, half],
        out_shape=[jax.ShapeDtypeStruct((heads, *shape), F32)] * 2,
        name="pack_q",
    )(seg, query, grad_out)


def unpack_q_kernel(outer_count, seg, low_ref, high_ref, out_ref):
    low, high = low_first(seg, outer_count, low_ref.shape[1])
    out_ref[low, :] = low_ref[0]
    out_ref[high, :] = high_ref[0]


def unpack_q(outer_count, seg, low, high):
    heads, stretch, width = low.shape
    half = pl.BlockSpec((1, stretch, width), lambda h: (h, 0, 0))
    return pl.pallas_call(
        functools.partial(unpack_q_kernel, outer_count),
        grid=(heads,),
        in_specs=[SMEM, half, half],
        out_specs=pl.BlockSpec((2 * stretch, width), lambda h: (0, h)),
        out_shape=jax.ShapeDtypeStruct((2 * stretch, heads * width), F32),
        name="unpack_q",
    )(seg, low, high)


def unpack_kv_kernel(outer_count, seg, d_ref, k_ref, v_ref):
    stretch = d_ref.shape[1] // 2
    for i, rows in enumerate(low_first(seg, outer_count, stretch)):
        at = slice(i * stretch, (i + 1) * stretch)
        for h in range(d_ref.shape[0]):
            columns = slice(h * HEAD_SIZE, (h + 1) * HEAD_SIZE)
            k_ref[rows, columns] = d_ref[h, at, :HEAD_SIZE]
            v_ref[rows, columns] = d_ref[h, at, HEAD_SIZE:]


def unpack_kv(outer_count, seg, dkv):
    heads, rows, _ = dkv.shape
    shape = (rows, heads * HEAD_SIZE)
    return pl.pallas_call(
        functools.partial(unpack_kv_kernel, outer_count),
        in_specs=[SMEM, pl.BlockSpec(dkv.shape, lambda: (0, 0, 0))],
        out_specs=[pl.BlockSpec(shape, lambda: (0, 0))] * 2,
        out_shape=[jax.ShapeDtypeStruct(shape, F32)] * 2,
        name="unpack_kv",
    )(seg, dkv)


def from_behind(x, axis, by):
    size = lax.axis_size(axis)
    return lax.ppermute(x, axis, [(i, (i + by) % size) for i in range(size)])


def in_order(later, earlier):
    return lax.optimization_barrier((later, earlier))


def local(query, keys, values, grad_out, segment_number):
    inner_count = lax.axis_size("inner")
    outer_count = lax.axis_size("outer")
    swap = lambda x: lax.all_to_all(x, "inner", 0, 0)
    seg = segment_number.T
    own = swap(pack_kv(outer_count, seg, keys, values, inner_count))
    q_low, q_high = pack_q(outer_count, seg, query, grad_out, inner_count)
    prev = from_behind(own, "outer", 1)
    q_high = swap(q_high)
    q_low, q_high = in_order(q_low, q_high)
    q_low = swap(q_low)
    dq_high, down, dprev = attention(True, outer_count, seg, q_high, own, prev)
    dq_high = swap(dq_high)
    dq_low, down, dprev = attention(False, outer_count, seg, q_low, own, prev, down, dprev)
    dq_low, dq_high = in_order(dq_low, dq_high)
    back = from_behind(dprev, "outer", -1)
    dq_low = swap(dq_low)
    dkv, dq_low = in_order(down + back, dq_low)
    dkv = swap(dkv)
    return (
        unpack_q(outer_count, seg, dq_low, dq_high),
        *unpack_kv(outer_count, seg, dkv),
    )


def solution(mesh):
    spec = P(("inner", "outer"), None)
    return jax.shard_map(
        local,
        mesh=mesh,
        in_specs=(spec, spec, spec, spec, P()),
        out_specs=(spec, spec, spec),
        check_vma=False,
    )
```

```python
import functools
import math

import jax
import jax.numpy as jnp
from jax import lax
from jax.experimental import pallas as pl
from jax.experimental.pallas import tpu as pltpu
from jax.sharding import PartitionSpec as P

ASKER_PLANES = 32
KEY_VALUE_HEADS = 8
HEAD_SIZE = 128
GROUP_LIST = ASKER_PLANES // KEY_VALUE_HEADS
HEAD_WIDTH = GROUP_LIST * HEAD_SIZE
TILE = 256
KEY_TILE = 256
SCORE_SCALE = HEAD_SIZE ** (-0.5)
LOG2E = math.log2(math.e)
F32 = jnp.float32
BF16 = jnp.bfloat16
SMEM = pl.BlockSpec(memory_space=pltpu.SMEM)
SMALL = pltpu.CompilerParams(vmem_limit_bytes=20 * 1024 * 1024)


def split2(x):
    high = x.astype(BF16)
    return high, (x - high.astype(F32)).astype(BF16)


def split3(x):
    high = x.astype(BF16)
    rest = x - high.astype(F32)
    middle = rest.astype(BF16)
    return high, middle, (rest - middle.astype(F32)).astype(BF16)


def dot(a, b):
    return jnp.dot(a, b, preferred_element_type=F32)


def fold(x, op):
    return op(x.reshape(x.shape[0] // 8, 8, x.shape[1]), axis=0)


def aligned(start, size):
    return pl.ds(pl.multiple_of(start, size), size)


def attention_kernel(inner_count, outer_count, is_high, seg, q_ref, own_ref, prev_ref, *refs):
    if is_high:
        dq_ref, down_ref, dprev_ref, *refs = refs
    else:
        down_in, dprev_in, dq_ref, down_ref, dprev_ref, *refs = refs
    rank, ksort, kcat, vcat, ktrans, dk_acc, dv_acc, s_scr, dp_scr, peaks = refs
    step = pl.program_id(0)
    blocks = 2 * inner_count
    stretch = q_ref.shape[2]
    per_tile = KEY_TILE // stretch

    def slots():
        for j in range(blocks):
            yield j, 0, rank[j]
            if is_high:
                yield j, 1, 2 * blocks - 1 - rank[j]

    @pl.when(step == 0)
    def _():
        outer = lax.axis_index("outer")
        before = lax.rem(outer + outer_count - 1, outer_count)
        lows = []
        for j in range(blocks):
            device = (j % inner_count) * outer_count + (outer if j < inner_count else before)
            lows.append(jnp.minimum(seg[0, device], seg[1, device]))
        for j in range(blocks):
            below = jnp.int32(0)
            for other in range(blocks):
                if other != j:
                    below = below + (lows[other] < lows[j]).astype(jnp.int32)
            rank[j] = below
        for j, half, slot in slots():
            ref, at = (own_ref, j) if j < inner_count else (prev_ref, j - inner_count)
            to = aligned(slot * stretch, stretch)
            both = ref[at, half * stretch : (half + 1) * stretch, :]
            key, value = both[:, :HEAD_SIZE], both[:, HEAD_SIZE:]
            ksort[to, :] = key
            h, m, l = split3(key)
            kcat[to, :] = jnp.concatenate([h, h, m, h, l, m], axis=1)
            h, l = split2(value)
            vcat[to, :] = jnp.concatenate([h, h, l, l], axis=1)
        for t in range(ksort.shape[0] // KEY_TILE):
            h, l = split2(ksort[t * KEY_TILE : (t + 1) * KEY_TILE, :].T)
            ktrans[t] = jnp.concatenate([h, l], axis=0)
        dk_acc[...] = jnp.zeros_like(dk_acc)
        dv_acc[...] = jnp.zeros_like(dv_acc)

    reach = 2 * blocks - 1 - rank[step] if is_high else rank[step]
    last = reach // per_tile
    heads = [slice(g * HEAD_SIZE, (g + 1) * HEAD_SIZE) for g in range(GROUP_LIST)]
    q = jnp.concatenate([q_ref[0, 0, :, g] for g in heads], axis=0) * (SCORE_SCALE * LOG2E)
    do = jnp.concatenate([q_ref[0, 1, :, g] for g in heads], axis=0)
    h, m, l = split3(q.T)
    qt = jnp.concatenate([h, m, h, l, h, m], axis=0)
    h, l = split2(q)
    q_pair = jnp.concatenate([h, l], axis=1)
    q_rhs = jnp.concatenate([q_pair, q_pair], axis=0)
    h, l = split2(do.T)
    dot_t = jnp.concatenate([h, l, h, l], axis=0)
    h, l = split2(do)
    do_pair = jnp.concatenate([h, l], axis=1)
    do_rhs = jnp.concatenate([do_pair, do_pair], axis=0)

    def open_tile(t, carry, visible=None):
        peak, total, delta = carry
        at = slice(t * KEY_TILE, (t + 1) * KEY_TILE)
        s = dot(kcat[at, :], qt)
        dp = dot(vcat[at, :], dot_t)
        if visible is not None:
            s = jnp.where(visible, s, -jnp.inf)
        higher = jnp.maximum(peak, jnp.max(s, axis=0, keepdims=True))
        e = jnp.exp2(s - higher)
        s_scr[at, :] = e
        dp_scr[at, :] = dp
        peaks[t] = higher
        shrink = jnp.exp2(peak - higher)
        total = total * shrink + jnp.sum(e, axis=0, keepdims=True)
        delta = delta * shrink + jnp.sum(e * dp, axis=0, keepdims=True)
        return higher, total, delta

    key_at = lax.broadcasted_iota(jnp.int32, (KEY_TILE, TILE), 0)
    token = lax.rem(lax.broadcasted_iota(jnp.int32, (KEY_TILE, TILE), 1), stretch)

    def whole(count):
        carry = (jnp.full((1, TILE), -jnp.inf, F32), *[jnp.zeros((1, TILE), F32)] * 2)
        for t in range(count):
            visible = None
            if t == count - 1:
                visible = key_at <= (reach - t * per_tile) * stretch + token
            carry = open_tile(t, carry, visible)
        peak, total, delta = carry
        inverse = 1.0 / total
        delta = delta * inverse
        dqt = dqt_low = None
        for t in range(count):
            at = slice(t * KEY_TILE, (t + 1) * KEY_TILE)
            p = s_scr[at, :] * (jnp.exp2(peaks[t] - peak) * inverse)
            ds = p * (dp_scr[at, :] - delta)
            dv_acc[at, :] += dot(jnp.concatenate(split2(p), axis=1), do_rhs)
            h, l = split2(ds)
            dk_acc[at, :] += dot(jnp.concatenate([h, l], axis=1), q_rhs)
            term = dot(ktrans[t], h)
            low_term = dot(ktrans[t, :HEAD_SIZE], l)
            dqt = term if dqt is None else dqt + term
            dqt_low = low_term if dqt_low is None else dqt_low + low_term
        dq = ((dqt[:HEAD_SIZE] + dqt[HEAD_SIZE:] + dqt_low) * SCORE_SCALE).T
        for i, g in enumerate(heads):
            dq_ref[0, :, g] = dq[i * stretch : (i + 1) * stretch]

    tiles = blocks // per_tile
    for count in range(tiles + 1, 2 * tiles + 1) if is_high else range(1, tiles + 1):
        pl.when(last == count - 1)(functools.partial(whole, count))

    @pl.when(step == pl.num_programs(0) - 1)
    def _():
        for j, half, slot in slots():
            came = aligned(slot * stretch, stretch)
            dk, dv = dk_acc[came, :], dv_acc[came, :]
            dk = (dk[:, :HEAD_SIZE] + dk[:, HEAD_SIZE:]) * (1.0 / LOG2E)
            dv = dv[:, :HEAD_SIZE] + dv[:, HEAD_SIZE:]
            is_own = j < inner_count
            at = j if is_own else j - inner_count
            ref = down_ref if is_own else dprev_ref
            rows = slice(half * stretch, (half + 1) * stretch)
            if not is_high:
                earlier = down_in if is_own else dprev_in
                dk = dk + earlier[at, rows, :HEAD_SIZE]
                dv = dv + earlier[at, rows, HEAD_SIZE:]
                ref[at, stretch:, :] = earlier[at, stretch:, :]
            ref[at, rows, :HEAD_SIZE] = dk
            ref[at, rows, HEAD_SIZE:] = dv


def attention(is_high, outer_count, seg, q, own, prev, *earlier):
    inner_count, rows, _ = own.shape
    stretch = rows // 2
    key_rows = rows if is_high else stretch
    keys = 2 * inner_count * key_rows
    whole = lambda r: pl.BlockSpec((inner_count, r, 2 * HEAD_SIZE), lambda i: (0, 0, 0))
    tiles = 52 if is_high else 20
    return pl.pallas_call(
        functools.partial(attention_kernel, inner_count, outer_count, is_high),
        grid=(inner_count,),
        in_specs=[
            SMEM,
            pl.BlockSpec((1, 2, stretch, HEAD_WIDTH), lambda i: (i, 0, 0, 0)),
            whole(key_rows), whole(key_rows),
        ] + [whole(rows)] * len(earlier),
        out_specs=[pl.BlockSpec((1, stretch, HEAD_WIDTH), lambda i: (i, 0, 0))] + [whole(rows)] * 2,
        out_shape=[jax.ShapeDtypeStruct((inner_count, stretch, HEAD_WIDTH), F32)] + [jax.ShapeDtypeStruct(own.shape, F32)] * 2,
        scratch_shapes=[
            pltpu.SMEM((2 * inner_count,), jnp.int32),
            pltpu.VMEM((keys, HEAD_SIZE), F32),
            pltpu.VMEM((keys, 6 * HEAD_SIZE), BF16),
            pltpu.VMEM((keys, 4 * HEAD_SIZE), BF16),
            pltpu.VMEM((keys // KEY_TILE, 2 * HEAD_SIZE, KEY_TILE), BF16),
            pltpu.VMEM((keys, 2 * HEAD_SIZE), F32),
            pltpu.VMEM((keys, 2 * HEAD_SIZE), F32),
            pltpu.VMEM((keys, TILE), F32),
            pltpu.VMEM((keys, TILE), F32),
            pltpu.VMEM((keys // KEY_TILE, 1, TILE), F32),
        ],
        cost_estimate=pl.CostEstimate(
            flops=tiles * 1_000_000_000, bytes_accessed=8 << 20, transcendentals=0
        ),
        compiler_params=pltpu.CompilerParams(vmem_limit_bytes=58 * 1024 * 1024),
        name="attention_high" if is_high else "attention_low",
    )(seg, q, own, prev, *earlier)


def low_first(seg, outer_count, stretch):
    device = lax.axis_index("inner") * outer_count + lax.axis_index("outer")
    low = jnp.where(seg[0, device] < seg[1, device], 0, stretch)
    return aligned(low, stretch), aligned(stretch - low, stretch)


def pack_kv_kernel(outer_count, seg, k_ref, v_ref, out_ref):
    stretch = k_ref.shape[0] // 2
    for i, rows in enumerate(low_first(seg, outer_count, stretch)):
        at = slice(i * stretch, (i + 1) * stretch)
        for h in range(out_ref.shape[0]):
            columns = slice(h * HEAD_SIZE, (h + 1) * HEAD_SIZE)
            out_ref[h, at, :HEAD_SIZE] = k_ref[rows, columns]
            out_ref[h, at, HEAD_SIZE:] = v_ref[rows, columns]


def pack_kv(outer_count, seg, keys, values, heads):
    rows, width = keys.shape
    whole = pl.BlockSpec((rows, width), lambda: (0, 0))
    shape = (heads, rows, 2 * HEAD_SIZE)
    return pl.pallas_call(
        functools.partial(pack_kv_kernel, outer_count),
        in_specs=[SMEM, whole, whole],
        out_specs=pl.BlockSpec(shape, lambda: (0, 0, 0)),
        out_shape=jax.ShapeDtypeStruct(shape, F32),
        name="pack_kv",
    )(seg, keys, values)


def pack_q_kernel(outer_count, seg, q_ref, do_ref, low_ref, high_ref):
    stretch = q_ref.shape[0] // 2
    low, high = low_first(seg, outer_count, stretch)
    low_ref[0, 0], low_ref[0, 1] = q_ref[low, :], do_ref[low, :]
    high_ref[0, 0], high_ref[0, 1] = q_ref[high, :], do_ref[high, :]


def pack_q(outer_count, seg, query, grad_out, heads):
    rows = query.shape[0]
    shape = (2, rows // 2, HEAD_WIDTH)
    half = pl.BlockSpec((1, *shape), lambda h: (h, 0, 0, 0))
    return pl.pallas_call(
        functools.partial(pack_q_kernel, outer_count),
        grid=(heads,),
        in_specs=[SMEM] + [pl.BlockSpec((rows, HEAD_WIDTH), lambda h: (0, h))] * 2,
        out_specs=[half, half],
        out_shape=[jax.ShapeDtypeStruct((heads, *shape), F32)] * 2,
        name="pack_q",
    )(seg, query, grad_out)


def unpack_q_kernel(outer_count, seg, low_ref, high_ref, out_ref):
    low, high = low_first(seg, outer_count, low_ref.shape[1])
    out_ref[low, :] = low_ref[0]
    out_ref[high, :] = high_ref[0]


def unpack_q(outer_count, seg, low, high):
    heads, stretch, width = low.shape
    half = pl.BlockSpec((1, stretch, width), lambda h: (h, 0, 0))
    return pl.pallas_call(
        functools.partial(unpack_q_kernel, outer_count),
        grid=(heads,),
        in_specs=[SMEM, half, half],
        out_specs=pl.BlockSpec((2 * stretch, width), lambda h: (0, h)),
        out_shape=jax.ShapeDtypeStruct((2 * stretch, heads * width), F32),
        compiler_params=SMALL,
        name="unpack_q",
    )(seg, low, high)


def partner(inner, offset, count, back=False):
    step = count - offset // 2 * 2 if back else offset // 2 * 2
    return (inner // 2 * 2 + step) % count + (inner % 2 + offset % 2) % 2


def combine_kernel(down_ref, back_ref, *out_refs):
    for offset, ref in enumerate(out_refs):
        to = partner(lax.axis_index("inner"), offset, len(out_refs))
        ref[...] = down_ref[to] + back_ref[to]


def spread(down, back):
    count, *shape = down.shape
    whole = pl.BlockSpec(down.shape, lambda: (0, 0, 0))
    blocks = pl.pallas_call(
        combine_kernel,
        in_specs=[whole, whole],
        out_specs=[pl.BlockSpec(shape, lambda: (0, 0))] * count,
        out_shape=[jax.ShapeDtypeStruct(shape, F32)] * count,
        compiler_params=SMALL,
        name="combine",
    )(down, back)
    to = lambda offset: [(i, partner(i, offset, count)) for i in range(count)]
    return [blocks[0]] + [lax.ppermute(blocks[s], "inner", to(s)) for s in range(1, count)]


def unpack_kv_kernel(outer_count, seg, *refs):
    *d_refs, k_ref, v_ref = refs
    stretch = k_ref.shape[0] // 2
    for i, rows in enumerate(low_first(seg, outer_count, stretch)):
        at = slice(i * stretch, (i + 1) * stretch)
        for offset, ref in enumerate(d_refs):
            head = partner(lax.axis_index("inner"), offset, len(d_refs), back=True)
            columns = aligned(head * HEAD_SIZE, HEAD_SIZE)
            k_ref[rows, columns] = ref[at, :HEAD_SIZE]
            v_ref[rows, columns] = ref[at, HEAD_SIZE:]


def unpack_kv(outer_count, seg, blocks):
    heads, rows = len(blocks), blocks[0].shape[0]
    shape = (rows, heads * HEAD_SIZE)
    return pl.pallas_call(
        functools.partial(unpack_kv_kernel, outer_count),
        in_specs=[SMEM] + [pl.BlockSpec(blocks[0].shape, lambda: (0, 0))] * heads,
        out_specs=[pl.BlockSpec(shape, lambda: (0, 0))] * 2,
        out_shape=[jax.ShapeDtypeStruct(shape, F32)] * 2,
        compiler_params=SMALL,
        name="unpack_kv",
    )(seg, *blocks)


def from_behind(x, axis, by):
    size = lax.axis_size(axis)
    return lax.ppermute(x, axis, [(i, (i + by) % size) for i in range(size)])


def in_order(later, earlier):
    return lax.optimization_barrier((later, earlier))


def local(query, keys, values, grad_out, segment_number):
    inner_count = lax.axis_size("inner")
    outer_count = lax.axis_size("outer")
    swap = lambda x: lax.all_to_all(x, "inner", 0, 0)
    seg = segment_number.T
    own = swap(pack_kv(outer_count, seg, keys, values, inner_count))
    q_low, q_high = pack_q(outer_count, seg, query, grad_out, inner_count)
    prev = from_behind(own, "outer", 1)
    q_high = swap(q_high)
    q_low, q_high = in_order(q_low, q_high)
    q_low = swap(q_low)
    dq_high, down, dprev = attention(True, outer_count, seg, q_high, own, prev)
    dq_high = swap(dq_high)
    dq_low, down, dprev = attention(False, outer_count, seg, q_low, own, prev, down, dprev)
    dq_low, dq_high = in_order(dq_low, dq_high)
    dq_low = swap(dq_low)
    back = from_behind(dprev, "outer", -1)
    dkv = spread(down, back)
    return (
        unpack_q(outer_count, seg, dq_low, dq_high),
        *unpack_kv(outer_count, seg, dkv),
    )


def solution(mesh):
    spec = P(("inner", "outer"), None)
    return jax.shard_map(
        local,
        mesh=mesh,
        in_specs=(spec, spec, spec, spec, P()),
        out_specs=(spec, spec, spec),
        check_vma=False,
    )
```

```python
import functools
import math

import jax
import jax.numpy as jnp
from jax import lax
from jax.experimental import pallas as pl
from jax.experimental.pallas import tpu as pltpu
from jax.sharding import PartitionSpec as P

ASKER_PLANES = 32
KEY_VALUE_HEADS = 8
HEAD_SIZE = 128
GROUP_LIST = ASKER_PLANES // KEY_VALUE_HEADS
HEAD_WIDTH = GROUP_LIST * HEAD_SIZE
KEY_TILE = 256
SCORE_SCALE = HEAD_SIZE ** (-0.5)
LOG2E = math.log2(math.e)
F32 = jnp.float32
BF16 = jnp.bfloat16
SMEM = pl.BlockSpec(memory_space=pltpu.SMEM)
SMALL = pltpu.CompilerParams(vmem_limit_bytes=20 * 1024 * 1024)


def split2(x):
    high = x.astype(BF16)
    return high, (x - high.astype(F32)).astype(BF16)


def split3(x):
    high = x.astype(BF16)
    rest = x - high.astype(F32)
    middle = rest.astype(BF16)
    return high, middle, (rest - middle.astype(F32)).astype(BF16)


def dot(a, b):
    return jnp.dot(a, b, preferred_element_type=F32)


def fold(x, op):
    return op(x.reshape(x.shape[0] // 8, 8, x.shape[1]), axis=0)


def aligned(start, size):
    return pl.ds(pl.multiple_of(start, size), size)


def attention_kernel(inner_count, outer_count, is_high, seg, q_ref, own_ref, prev_ref, *refs):
    if is_high:
        dq_ref, down_ref, dprev_ref, *refs = refs
    else:
        down_in, dprev_in, dq_ref, down_ref, dprev_ref, *refs = refs
    rank, order, ksort, kcat, vcat, ktrans, dk_acc, dv_acc, s_scr, dp_scr, peaks = refs
    blocks = 2 * inner_count
    stretch = q_ref.shape[2]
    per_tile = KEY_TILE // stretch

    def slots():
        for j in range(blocks):
            yield j, 0, rank[j]
            if is_high:
                yield j, 1, 2 * blocks - 1 - rank[j]

    outer = lax.axis_index("outer")
    before = lax.rem(outer + outer_count - 1, outer_count)
    lows = []
    for j in range(blocks):
        device = (j % inner_count) * outer_count + (outer if j < inner_count else before)
        lows.append(jnp.minimum(seg[0, device], seg[1, device]))
    for j in range(blocks):
        below = jnp.int32(0)
        for other in range(blocks):
            if other != j:
                below = below + (lows[other] < lows[j]).astype(jnp.int32)
        rank[j] = below
    for j in range(inner_count):
        below = jnp.int32(0)
        for other in range(inner_count):
            if other != j:
                below = below + (lows[other] < lows[j]).astype(jnp.int32)
        order[below] = j
    for j, half, slot in slots():
        ref, at = (own_ref, j) if j < inner_count else (prev_ref, j - inner_count)
        to = aligned(slot * stretch, stretch)
        both = ref[at, half * stretch : (half + 1) * stretch, :]
        key, value = both[:, :HEAD_SIZE], both[:, HEAD_SIZE:]
        ksort[to, :] = key
        h, m, l = split3(key)
        kcat[to, :] = jnp.concatenate([h, h, m, h, l, m], axis=1)
        h, l = split2(value)
        vcat[to, :] = jnp.concatenate([h, h, l, l], axis=1)
    for t in range(ksort.shape[0] // KEY_TILE):
        h, l = split2(ksort[t * KEY_TILE : (t + 1) * KEY_TILE, :].T)
        ktrans[t] = jnp.concatenate([h, l], axis=0)
    dk_acc[...] = jnp.zeros_like(dk_acc)
    dv_acc[...] = jnp.zeros_like(dv_acc)

    heads = [slice(g * HEAD_SIZE, (g + 1) * HEAD_SIZE) for g in range(GROUP_LIST)]
    columns = 2 * GROUP_LIST * stretch
    column = lax.broadcasted_iota(jnp.int32, (1, columns), 1)
    token = lax.rem(column, stretch)
    key_at = lax.broadcasted_iota(jnp.int32, (KEY_TILE, 1), 0)
    tiles = blocks // per_tile

    def pair(step, _):
        ids = [order[2 * step], order[2 * step + 1]]
        reaches = [2 * blocks - 1 - rank[i] if is_high else rank[i] for i in ids]
        limit = jnp.where(column < columns // 2, *reaches) * stretch + token
        last = jnp.maximum(*reaches) // per_tile
        q = jnp.concatenate([q_ref[i, 0, :, g] for i in ids for g in heads], axis=0) * (SCORE_SCALE * LOG2E)
        do = jnp.concatenate([q_ref[i, 1, :, g] for i in ids for g in heads], axis=0)
        h, m, l = split3(q.T)
        qt = jnp.concatenate([h, m, h, l, h, m], axis=0)
        h, l = split2(q)
        q_pair = jnp.concatenate([h, l], axis=1)
        q_rhs = jnp.concatenate([q_pair, q_pair], axis=0)
        h, l = split2(do.T)
        dot_t = jnp.concatenate([h, l, h, l], axis=0)
        h, l = split2(do)
        do_pair = jnp.concatenate([h, l], axis=1)
        do_rhs = jnp.concatenate([do_pair, do_pair], axis=0)

        def whole(count):
            peak = jnp.full((1, columns), -jnp.inf, F32)
            total = delta = jnp.zeros((1, columns), F32)
            for t in range(count):
                at = slice(t * KEY_TILE, (t + 1) * KEY_TILE)
                s = dot(kcat[at, :], qt)
                dp = dot(vcat[at, :], dot_t)
                if t >= tiles or not is_high:
                    s = jnp.where(key_at + t * KEY_TILE <= limit, s, -jnp.inf)
                higher = jnp.maximum(peak, jnp.max(s, axis=0, keepdims=True))
                e = jnp.exp2(s - higher)
                s_scr[at, :] = e
                dp_scr[at, :] = dp
                peaks[t] = higher
                shrink = jnp.exp2(peak - higher)
                total = total * shrink + jnp.sum(e, axis=0, keepdims=True)
                delta = delta * shrink + jnp.sum(e * dp, axis=0, keepdims=True)
                peak = higher
            inverse = 1.0 / total
            delta = delta * inverse
            dqt = dqt_low = None
            for t in range(count):
                at = slice(t * KEY_TILE, (t + 1) * KEY_TILE)
                p = s_scr[at, :] * (jnp.exp2(peaks[t] - peak) * inverse)
                ds = p * (dp_scr[at, :] - delta)
                dv_acc[at, :] += dot(jnp.concatenate(split2(p), axis=1), do_rhs)
                h, l = split2(ds)
                dk_acc[at, :] += dot(jnp.concatenate([h, l], axis=1), q_rhs)
                term = dot(ktrans[t], h)
                low_term = dot(ktrans[t, :HEAD_SIZE], l)
                dqt = term if dqt is None else dqt + term
                dqt_low = low_term if dqt_low is None else dqt_low + low_term
            dq = ((dqt[:HEAD_SIZE] + dqt[HEAD_SIZE:] + dqt_low) * SCORE_SCALE).T
            for n, i in enumerate(ids):
                for k, g in enumerate(heads):
                    first = (n * GROUP_LIST + k) * stretch
                    dq_ref[i, :, g] = dq[first : first + stretch]

        for count in range(tiles + 1, 2 * tiles + 1) if is_high else range(1, tiles + 1):
            pl.when(last == count - 1)(functools.partial(whole, count))
        return 0

    lax.fori_loop(0, inner_count // 2, pair, 0)

    for j, half, slot in slots():
        came = aligned(slot * stretch, stretch)
        dk, dv = dk_acc[came, :], dv_acc[came, :]
        dk = (dk[:, :HEAD_SIZE] + dk[:, HEAD_SIZE:]) * (1.0 / LOG2E)
        dv = dv[:, :HEAD_SIZE] + dv[:, HEAD_SIZE:]
        is_own = j < inner_count
        at = j if is_own else j - inner_count
        ref = down_ref if is_own else dprev_ref
        rows = slice(half * stretch, (half + 1) * stretch)
        if not is_high:
            earlier = down_in if is_own else dprev_in
            dk = dk + earlier[at, rows, :HEAD_SIZE]
            dv = dv + earlier[at, rows, HEAD_SIZE:]
            ref[at, stretch:, :] = earlier[at, stretch:, :]
        ref[at, rows, :HEAD_SIZE] = dk
        ref[at, rows, HEAD_SIZE:] = dv


def attention(is_high, outer_count, seg, q, own, prev, *earlier):
    inner_count, rows, _ = own.shape
    stretch = rows // 2
    key_rows = rows if is_high else stretch
    keys = 2 * inner_count * key_rows
    whole = lambda r: pl.BlockSpec((inner_count, r, 2 * HEAD_SIZE), lambda i: (0, 0, 0))
    columns = 2 * GROUP_LIST * stretch
    tiles = 52 if is_high else 20
    return pl.pallas_call(
        functools.partial(attention_kernel, inner_count, outer_count, is_high),
        grid=(1,),
        in_specs=[
            SMEM,
            pl.BlockSpec(q.shape, lambda i: (0, 0, 0, 0)),
            whole(key_rows), whole(key_rows),
        ] + [whole(rows)] * len(earlier),
        out_specs=[pl.BlockSpec((inner_count, stretch, HEAD_WIDTH), lambda i: (0, 0, 0))] + [whole(rows)] * 2,
        out_shape=[jax.ShapeDtypeStruct((inner_count, stretch, HEAD_WIDTH), F32)] + [jax.ShapeDtypeStruct(own.shape, F32)] * 2,
        scratch_shapes=[
            pltpu.SMEM((2 * inner_count,), jnp.int32),
            pltpu.SMEM((inner_count,), jnp.int32),
            pltpu.VMEM((keys, HEAD_SIZE), F32),
            pltpu.VMEM((keys, 6 * HEAD_SIZE), BF16),
            pltpu.VMEM((keys, 4 * HEAD_SIZE), BF16),
            pltpu.VMEM((keys // KEY_TILE, 2 * HEAD_SIZE, KEY_TILE), BF16),
            pltpu.VMEM((keys, 2 * HEAD_SIZE), F32),
            pltpu.VMEM((keys, 2 * HEAD_SIZE), F32),
            pltpu.VMEM((keys, columns), F32),
            pltpu.VMEM((keys, columns), F32),
            pltpu.VMEM((keys // KEY_TILE, 1, columns), F32),
        ],
        cost_estimate=pl.CostEstimate(
            flops=tiles * 1_000_000_000, bytes_accessed=8 << 20, transcendentals=0
        ),
        compiler_params=pltpu.CompilerParams(vmem_limit_bytes=58 * 1024 * 1024),
        name="attention_high" if is_high else "attention_low",
    )(seg, q, own, prev, *earlier)


def low_first(seg, outer_count, stretch):
    device = lax.axis_index("inner") * outer_count + lax.axis_index("outer")
    low = jnp.where(seg[0, device] < seg[1, device], 0, stretch)
    return aligned(low, stretch), aligned(stretch - low, stretch)


def pack_kv_kernel(outer_count, seg, k_ref, v_ref, out_ref):
    stretch = k_ref.shape[0] // 2
    for i, rows in enumerate(low_first(seg, outer_count, stretch)):
        at = slice(i * stretch, (i + 1) * stretch)
        for h in range(out_ref.shape[0]):
            columns = slice(h * HEAD_SIZE, (h + 1) * HEAD_SIZE)
            out_ref[h, at, :HEAD_SIZE] = k_ref[rows, columns]
            out_ref[h, at, HEAD_SIZE:] = v_ref[rows, columns]


def pack_kv(outer_count, seg, keys, values, heads):
    rows, width = keys.shape
    whole = pl.BlockSpec((rows, width), lambda: (0, 0))
    shape = (heads, rows, 2 * HEAD_SIZE)
    return pl.pallas_call(
        functools.partial(pack_kv_kernel, outer_count),
        in_specs=[SMEM, whole, whole],
        out_specs=pl.BlockSpec(shape, lambda: (0, 0, 0)),
        out_shape=jax.ShapeDtypeStruct(shape, F32),
        name="pack_kv",
    )(seg, keys, values)


def pack_q_kernel(outer_count, seg, q_ref, do_ref, low_ref, high_ref):
    stretch = q_ref.shape[0] // 2
    low, high = low_first(seg, outer_count, stretch)
    low_ref[0, 0], low_ref[0, 1] = q_ref[low, :], do_ref[low, :]
    high_ref[0, 0], high_ref[0, 1] = q_ref[high, :], do_ref[high, :]


def pack_q(outer_count, seg, query, grad_out, heads):
    rows = query.shape[0]
    shape = (2, rows // 2, HEAD_WIDTH)
    half = pl.BlockSpec((1, *shape), lambda h: (h, 0, 0, 0))
    return pl.pallas_call(
        functools.partial(pack_q_kernel, outer_count),
        grid=(heads,),
        in_specs=[SMEM] + [pl.BlockSpec((rows, HEAD_WIDTH), lambda h: (0, h))] * 2,
        out_specs=[half, half],
        out_shape=[jax.ShapeDtypeStruct((heads, *shape), F32)] * 2,
        name="pack_q",
    )(seg, query, grad_out)


def unpack_q_kernel(outer_count, seg, low_ref, high_ref, out_ref):
    low, high = low_first(seg, outer_count, low_ref.shape[1])
    out_ref[low, :] = low_ref[0]
    out_ref[high, :] = high_ref[0]


def unpack_q(outer_count, seg, low, high):
    heads, stretch, width = low.shape
    half = pl.BlockSpec((1, stretch, width), lambda h: (h, 0, 0))
    return pl.pallas_call(
        functools.partial(unpack_q_kernel, outer_count),
        grid=(heads,),
        in_specs=[SMEM, half, half],
        out_specs=pl.BlockSpec((2 * stretch, width), lambda h: (0, h)),
        out_shape=jax.ShapeDtypeStruct((2 * stretch, heads * width), F32),
        compiler_params=SMALL,
        name="unpack_q",
    )(seg, low, high)


def partner(inner, offset, count, back=False):
    step = count - offset // 2 * 2 if back else offset // 2 * 2
    return (inner // 2 * 2 + step) % count + (inner % 2 + offset % 2) % 2


def combine_kernel(down_ref, back_ref, *out_refs):
    for offset, ref in enumerate(out_refs):
        to = partner(lax.axis_index("inner"), offset, len(out_refs))
        ref[...] = down_ref[to] + back_ref[to]


def spread(down, back):
    count, *shape = down.shape
    whole = pl.BlockSpec(down.shape, lambda: (0, 0, 0))
    blocks = pl.pallas_call(
        combine_kernel,
        in_specs=[whole, whole],
        out_specs=[pl.BlockSpec(shape, lambda: (0, 0))] * count,
        out_shape=[jax.ShapeDtypeStruct(shape, F32)] * count,
        compiler_params=SMALL,
        name="combine",
    )(down, back)
    to = lambda offset: [(i, partner(i, offset, count)) for i in range(count)]
    return [blocks[0]] + [lax.ppermute(blocks[s], "inner", to(s)) for s in range(1, count)]


def unpack_kv_kernel(outer_count, seg, *refs):
    *d_refs, k_ref, v_ref = refs
    stretch = k_ref.shape[0] // 2
    for i, rows in enumerate(low_first(seg, outer_count, stretch)):
        at = slice(i * stretch, (i + 1) * stretch)
        for offset, ref in enumerate(d_refs):
            head = partner(lax.axis_index("inner"), offset, len(d_refs), back=True)
            columns = aligned(head * HEAD_SIZE, HEAD_SIZE)
            k_ref[rows, columns] = ref[at, :HEAD_SIZE]
            v_ref[rows, columns] = ref[at, HEAD_SIZE:]


def unpack_kv(outer_count, seg, blocks):
    heads, rows = len(blocks), blocks[0].shape[0]
    shape = (rows, heads * HEAD_SIZE)
    return pl.pallas_call(
        functools.partial(unpack_kv_kernel, outer_count),
        in_specs=[SMEM] + [pl.BlockSpec(blocks[0].shape, lambda: (0, 0))] * heads,
        out_specs=[pl.BlockSpec(shape, lambda: (0, 0))] * 2,
        out_shape=[jax.ShapeDtypeStruct(shape, F32)] * 2,
        compiler_params=SMALL,
        name="unpack_kv",
    )(seg, *blocks)


def from_behind(x, axis, by):
    size = lax.axis_size(axis)
    return lax.ppermute(x, axis, [(i, (i + by) % size) for i in range(size)])


def in_order(later, earlier):
    return lax.optimization_barrier((later, earlier))


def local(query, keys, values, grad_out, segment_number):
    inner_count = lax.axis_size("inner")
    outer_count = lax.axis_size("outer")
    swap = lambda x: lax.all_to_all(x, "inner", 0, 0)
    seg = segment_number.T
    own = swap(pack_kv(outer_count, seg, keys, values, inner_count))
    q_low, q_high = pack_q(outer_count, seg, query, grad_out, inner_count)
    prev = from_behind(own, "outer", 1)
    q_high = swap(q_high)
    q_low, q_high = in_order(q_low, q_high)
    q_low = swap(q_low)
    dq_high, down, dprev = attention(True, outer_count, seg, q_high, own, prev)
    dq_high = swap(dq_high)
    dq_low, down, dprev = attention(False, outer_count, seg, q_low, own, prev, down, dprev)
    dq_low, dq_high = in_order(dq_low, dq_high)
    dq_low = swap(dq_low)
    back = from_behind(dprev, "outer", -1)
    dkv = spread(down, back)
    return (
        unpack_q(outer_count, seg, dq_low, dq_high),
        *unpack_kv(outer_count, seg, dkv),
    )


def solution(mesh):
    spec = P(("inner", "outer"), None)
    return jax.shard_map(
        local,
        mesh=mesh,
        in_specs=(spec, spec, spec, spec, P()),
        out_specs=(spec, spec, spec),
        check_vma=False,
    )
```

```python
import functools
import math

import jax
import jax.numpy as jnp
from jax import lax
from jax.experimental import pallas as pl
from jax.experimental.pallas import tpu as pltpu
from jax.sharding import PartitionSpec as P

ASKER_PLANES = 32
KEY_VALUE_HEADS = 8
HEAD_SIZE = 128
GROUP_LIST = ASKER_PLANES // KEY_VALUE_HEADS
HEAD_WIDTH = GROUP_LIST * HEAD_SIZE
KEY_TILE = 256
SCORE_SCALE = HEAD_SIZE ** (-0.5)
LOG2E = math.log2(math.e)
F32 = jnp.float32
BF16 = jnp.bfloat16
SMEM = pl.BlockSpec(memory_space=pltpu.SMEM)
SMALL = pltpu.CompilerParams(vmem_limit_bytes=20 * 1024 * 1024)


def split2(x):
    high = x.astype(BF16)
    return high, (x - high.astype(F32)).astype(BF16)


def split3(x):
    high = x.astype(BF16)
    rest = x - high.astype(F32)
    middle = rest.astype(BF16)
    return high, middle, (rest - middle.astype(F32)).astype(BF16)


def dot(a, b):
    return jnp.dot(a, b, preferred_element_type=F32)


def fold(x, op):
    return op(x.reshape(x.shape[0] // 8, 8, x.shape[1]), axis=0)


def aligned(start, size):
    return pl.ds(pl.multiple_of(start, size), size)


def attention_kernel(inner_count, outer_count, is_high, seg, q_ref, own_ref, prev_ref, *refs):
    if is_high:
        dq_ref, down_ref, dprev_ref, *refs = refs
    else:
        down_in, dprev_in, dq_ref, down_ref, dprev_ref, *refs = refs
    rank, order, ksort, kcat, vcat, ktrans, dk_acc, dv_acc, s_scr, dp_scr, peaks = refs
    blocks = 2 * inner_count
    stretch = q_ref.shape[2]
    per_tile = KEY_TILE // stretch

    def slots():
        for j in range(blocks):
            yield j, 0, rank[j]
            if is_high:
                yield j, 1, 2 * blocks - 1 - rank[j]

    outer = lax.axis_index("outer")
    before = lax.rem(outer + outer_count - 1, outer_count)
    lows = []
    for j in range(blocks):
        device = (j % inner_count) * outer_count + (outer if j < inner_count else before)
        lows.append(jnp.minimum(seg[0, device], seg[1, device]))
    for j in range(blocks):
        below = jnp.int32(0)
        for other in range(blocks):
            if other != j:
                below = below + (lows[other] < lows[j]).astype(jnp.int32)
        rank[j] = below
    for j in range(inner_count):
        below = jnp.int32(0)
        for other in range(inner_count):
            if other != j:
                below = below + (lows[other] < lows[j]).astype(jnp.int32)
        order[below] = j
    for j, half, slot in slots():
        ref, at = (own_ref, j) if j < inner_count else (prev_ref, j - inner_count)
        to = aligned(slot * stretch, stretch)
        both = ref[at, half * stretch : (half + 1) * stretch, :]
        key, value = both[:, :HEAD_SIZE], both[:, HEAD_SIZE:]
        ksort[to, :] = key
        h, m, l = split3(key)
        kcat[to, :] = jnp.concatenate([h, h, m, h, l, m], axis=1)
        h, l = split2(value)
        vcat[to, :] = jnp.concatenate([h, h, l, l], axis=1)
    for t in range(ksort.shape[0] // KEY_TILE):
        h, l = split2(ksort[t * KEY_TILE : (t + 1) * KEY_TILE, :].T)
        ktrans[t] = jnp.concatenate([h, l], axis=0)
    dk_acc[...] = jnp.zeros_like(dk_acc)
    dv_acc[...] = jnp.zeros_like(dv_acc)

    heads = [slice(g * HEAD_SIZE, (g + 1) * HEAD_SIZE) for g in range(GROUP_LIST)]
    columns = 2 * GROUP_LIST * stretch
    column = lax.broadcasted_iota(jnp.int32, (1, columns), 1)
    token = lax.rem(column, stretch)
    key_at = lax.broadcasted_iota(jnp.int32, (KEY_TILE, 1), 0)
    tiles = blocks // per_tile

    def pair(step, _):
        ids = [order[2 * step], order[2 * step + 1]]
        reaches = [2 * blocks - 1 - rank[i] if is_high else rank[i] for i in ids]
        limit = jnp.where(column < columns // 2, *reaches) * stretch + token
        last = jnp.maximum(*reaches) // per_tile
        q = jnp.concatenate([q_ref[i, 0, :, g] for i in ids for g in heads], axis=0) * (SCORE_SCALE * LOG2E)
        do = jnp.concatenate([q_ref[i, 1, :, g] for i in ids for g in heads], axis=0)
        h, m, l = split3(q.T)
        qt = jnp.concatenate([h, m, h, l, h, m], axis=0)
        h, l = split2(q)
        q_pair = jnp.concatenate([h, l], axis=1)
        q_rhs = jnp.concatenate([q_pair, q_pair], axis=0)
        h, l = split2(do.T)
        dot_t = jnp.concatenate([h, l, h, l], axis=0)
        h, l = split2(do)
        do_pair = jnp.concatenate([h, l], axis=1)
        do_rhs = jnp.concatenate([do_pair, do_pair], axis=0)

        def whole(count):
            peak = jnp.full((1, columns), -jnp.inf, F32)
            total = delta = jnp.zeros((1, columns), F32)
            for t in range(count):
                at = slice(t * KEY_TILE, (t + 1) * KEY_TILE)
                s = dot(kcat[at, :], qt)
                dp = dot(vcat[at, :], dot_t)
                if t >= tiles or not is_high:
                    s = jnp.where(key_at + t * KEY_TILE <= limit, s, -jnp.inf)
                higher = jnp.maximum(peak, jnp.max(s, axis=0, keepdims=True))
                e = jnp.exp2(s - higher)
                s_scr[at, :] = e
                dp_scr[at, :] = dp
                peaks[t] = higher
                shrink = jnp.exp2(peak - higher)
                total = total * shrink + jnp.sum(e, axis=0, keepdims=True)
                delta = delta * shrink + jnp.sum(e * dp, axis=0, keepdims=True)
                peak = higher
            inverse = 1.0 / total
            delta = delta * inverse
            dqt = dqt_low = None
            for t in range(count):
                at = slice(t * KEY_TILE, (t + 1) * KEY_TILE)
                p = s_scr[at, :] * (jnp.exp2(peaks[t] - peak) * inverse)
                ds = p * (dp_scr[at, :] - delta)
                dv_acc[at, :] += dot(jnp.concatenate(split2(p), axis=1), do_rhs)
                h, l = split2(ds)
                dk_acc[at, :] += dot(jnp.concatenate([h, l], axis=1), q_rhs)
                term = dot(ktrans[t], h)
                low_term = dot(ktrans[t, :HEAD_SIZE], l)
                dqt = term if dqt is None else dqt + term
                dqt_low = low_term if dqt_low is None else dqt_low + low_term
            dq = ((dqt[:HEAD_SIZE] + dqt[HEAD_SIZE:] + dqt_low) * SCORE_SCALE).T
            for n, i in enumerate(ids):
                for k, g in enumerate(heads):
                    first = (n * GROUP_LIST + k) * stretch
                    dq_ref[i, :, g] = dq[first : first + stretch]

        for count in range(tiles + 1, 2 * tiles + 1) if is_high else range(1, tiles + 1):
            pl.when(last == count - 1)(functools.partial(whole, count))
        return 0

    lax.fori_loop(0, inner_count // 2, pair, 0)

    for j, half, slot in slots():
        came = aligned(slot * stretch, stretch)
        dk, dv = dk_acc[came, :], dv_acc[came, :]
        dk = (dk[:, :HEAD_SIZE] + dk[:, HEAD_SIZE:]) * (1.0 / LOG2E)
        dv = dv[:, :HEAD_SIZE] + dv[:, HEAD_SIZE:]
        is_own = j < inner_count
        at = j if is_own else j - inner_count
        ref = down_ref if is_own else dprev_ref
        rows = slice(half * stretch, (half + 1) * stretch)
        if not is_high:
            earlier = down_in if is_own else dprev_in
            dk = dk + earlier[at, rows, :HEAD_SIZE]
            dv = dv + earlier[at, rows, HEAD_SIZE:]
            ref[at, stretch:, :] = earlier[at, stretch:, :]
        ref[at, rows, :HEAD_SIZE] = dk
        ref[at, rows, HEAD_SIZE:] = dv


def attention(is_high, outer_count, seg, q, own, prev, *earlier):
    inner_count, rows, _ = own.shape
    stretch = rows // 2
    key_rows = rows if is_high else stretch
    keys = 2 * inner_count * key_rows
    whole = lambda r: pl.BlockSpec((inner_count, r, 2 * HEAD_SIZE), lambda i: (0, 0, 0))
    columns = 2 * GROUP_LIST * stretch
    tiles = 52 if is_high else 20
    return pl.pallas_call(
        functools.partial(attention_kernel, inner_count, outer_count, is_high),
        grid=(1,),
        in_specs=[
            SMEM,
            pl.BlockSpec(q.shape, lambda i: (0, 0, 0, 0)),
            whole(key_rows), whole(key_rows),
        ] + [whole(rows)] * len(earlier),
        out_specs=[pl.BlockSpec((inner_count, stretch, HEAD_WIDTH), lambda i: (0, 0, 0))] + [whole(rows)] * 2,
        out_shape=[jax.ShapeDtypeStruct((inner_count, stretch, HEAD_WIDTH), F32)] + [jax.ShapeDtypeStruct(own.shape, F32)] * 2,
        scratch_shapes=[
            pltpu.SMEM((2 * inner_count,), jnp.int32),
            pltpu.SMEM((inner_count,), jnp.int32),
            pltpu.VMEM((keys, HEAD_SIZE), F32),
            pltpu.VMEM((keys, 6 * HEAD_SIZE), BF16),
            pltpu.VMEM((keys, 4 * HEAD_SIZE), BF16),
            pltpu.VMEM((keys // KEY_TILE, 2 * HEAD_SIZE, KEY_TILE), BF16),
            pltpu.VMEM((keys, 2 * HEAD_SIZE), F32),
            pltpu.VMEM((keys, 2 * HEAD_SIZE), F32),
            pltpu.VMEM((keys, columns), F32),
            pltpu.VMEM((keys, columns), F32),
            pltpu.VMEM((keys // KEY_TILE, 1, columns), F32),
        ],
        cost_estimate=pl.CostEstimate(
            flops=tiles * 1_000_000_000, bytes_accessed=8 << 20, transcendentals=0
        ),
        compiler_params=pltpu.CompilerParams(vmem_limit_bytes=58 * 1024 * 1024),
        name="attention_high" if is_high else "attention_low",
    )(seg, q, own, prev, *earlier)


def low_first(seg, outer_count, stretch):
    device = lax.axis_index("inner") * outer_count + lax.axis_index("outer")
    low = jnp.where(seg[0, device] < seg[1, device], 0, stretch)
    return aligned(low, stretch), aligned(stretch - low, stretch)


def pack_kv_kernel(outer_count, seg, k_ref, v_ref, out_ref):
    stretch = k_ref.shape[0] // 2
    for i, rows in enumerate(low_first(seg, outer_count, stretch)):
        at = slice(i * stretch, (i + 1) * stretch)
        for h in range(out_ref.shape[0]):
            columns = slice(h * HEAD_SIZE, (h + 1) * HEAD_SIZE)
            out_ref[h, at, :HEAD_SIZE] = k_ref[rows, columns]
            out_ref[h, at, HEAD_SIZE:] = v_ref[rows, columns]


def pack_kv(outer_count, seg, keys, values, heads):
    rows, width = keys.shape
    some = pl.BlockSpec((rows, width // 2), lambda i: (0, i))
    return pl.pallas_call(
        functools.partial(pack_kv_kernel, outer_count),
        grid=(2,),
        in_specs=[SMEM, some, some],
        out_specs=pl.BlockSpec((heads // 2, rows, 2 * HEAD_SIZE), lambda i: (i, 0, 0)),
        out_shape=jax.ShapeDtypeStruct((heads, rows, 2 * HEAD_SIZE), F32),
        name="pack_kv",
    )(seg, keys, values)


def pack_q_kernel(outer_count, seg, q_ref, do_ref, low_ref, high_ref):
    stretch = q_ref.shape[0] // 2
    low, high = low_first(seg, outer_count, stretch)
    low_ref[0, 0], low_ref[0, 1] = q_ref[low, :], do_ref[low, :]
    high_ref[0, 0], high_ref[0, 1] = q_ref[high, :], do_ref[high, :]


def pack_q(outer_count, seg, query, grad_out, heads):
    rows = query.shape[0]
    shape = (2, rows // 2, HEAD_WIDTH)
    half = pl.BlockSpec((1, *shape), lambda h: (h, 0, 0, 0))
    return pl.pallas_call(
        functools.partial(pack_q_kernel, outer_count),
        grid=(heads,),
        in_specs=[SMEM] + [pl.BlockSpec((rows, HEAD_WIDTH), lambda h: (0, h))] * 2,
        out_specs=[half, half],
        out_shape=[jax.ShapeDtypeStruct((heads, *shape), F32)] * 2,
        name="pack_q",
    )(seg, query, grad_out)


def unpack_q_kernel(outer_count, seg, low_ref, high_ref, out_ref):
    low, high = low_first(seg, outer_count, low_ref.shape[1])
    out_ref[low, :] = low_ref[0]
    out_ref[high, :] = high_ref[0]


def unpack_q(outer_count, seg, low, high):
    heads, stretch, width = low.shape
    half = pl.BlockSpec((1, stretch, width), lambda h: (h, 0, 0))
    return pl.pallas_call(
        functools.partial(unpack_q_kernel, outer_count),
        grid=(heads,),
        in_specs=[SMEM, half, half],
        out_specs=pl.BlockSpec((2 * stretch, width), lambda h: (0, h)),
        out_shape=jax.ShapeDtypeStruct((2 * stretch, heads * width), F32),
        compiler_params=SMALL,
        name="unpack_q",
    )(seg, low, high)


def partner(inner, offset, count, back=False):
    step = count - offset // 2 * 2 if back else offset // 2 * 2
    return (inner // 2 * 2 + step) % count + (inner % 2 + offset % 2) % 2


def combine_kernel(down_ref, back_ref, *out_refs):
    for offset, ref in enumerate(out_refs):
        to = partner(lax.axis_index("inner"), offset, len(out_refs))
        ref[...] = down_ref[to] + back_ref[to]


def spread(down, back):
    count, *shape = down.shape
    whole = pl.BlockSpec(down.shape, lambda: (0, 0, 0))
    blocks = pl.pallas_call(
        combine_kernel,
        in_specs=[whole, whole],
        out_specs=[pl.BlockSpec(shape, lambda: (0, 0))] * count,
        out_shape=[jax.ShapeDtypeStruct(shape, F32)] * count,
        compiler_params=SMALL,
        name="combine",
    )(down, back)
    to = lambda offset: [(i, partner(i, offset, count)) for i in range(count)]
    return [blocks[0]] + [lax.ppermute(blocks[s], "inner", to(s)) for s in range(1, count)]


def unpack_kv_kernel(outer_count, seg, *refs):
    *d_refs, k_ref, v_ref = refs
    stretch = k_ref.shape[0] // 2
    for i, rows in enumerate(low_first(seg, outer_count, stretch)):
        at = slice(i * stretch, (i + 1) * stretch)
        for offset, ref in enumerate(d_refs):
            head = partner(lax.axis_index("inner"), offset, len(d_refs), back=True)
            columns = aligned(head * HEAD_SIZE, HEAD_SIZE)
            k_ref[rows, columns] = ref[at, :HEAD_SIZE]
            v_ref[rows, columns] = ref[at, HEAD_SIZE:]


def unpack_kv(outer_count, seg, blocks):
    heads, rows = len(blocks), blocks[0].shape[0]
    shape = (rows, heads * HEAD_SIZE)
    return pl.pallas_call(
        functools.partial(unpack_kv_kernel, outer_count),
        in_specs=[SMEM] + [pl.BlockSpec(blocks[0].shape, lambda: (0, 0))] * heads,
        out_specs=[pl.BlockSpec(shape, lambda: (0, 0))] * 2,
        out_shape=[jax.ShapeDtypeStruct(shape, F32)] * 2,
        compiler_params=SMALL,
        name="unpack_kv",
    )(seg, *blocks)


def from_behind(x, axis, by):
    size = lax.axis_size(axis)
    return lax.ppermute(x, axis, [(i, (i + by) % size) for i in range(size)])


def in_order(later, earlier):
    return lax.optimization_barrier((later, earlier))


def local(query, keys, values, grad_out, segment_number):
    inner_count = lax.axis_size("inner")
    outer_count = lax.axis_size("outer")
    swap = lambda x: lax.all_to_all(x, "inner", 0, 0)
    seg = segment_number.T
    own = swap(pack_kv(outer_count, seg, keys, values, inner_count))
    q_low, q_high = pack_q(outer_count, seg, query, grad_out, inner_count)
    prev = from_behind(own, "outer", 1)
    q_high = swap(q_high)
    q_low, q_high = in_order(q_low, q_high)
    q_low = swap(q_low)
    dq_high, down, dprev = attention(True, outer_count, seg, q_high, own, prev)
    dq_high = swap(dq_high)
    dq_low, down, dprev = attention(False, outer_count, seg, q_low, own, prev, down, dprev)
    dq_low, dq_high = in_order(dq_low, dq_high)
    dq_low = swap(dq_low)
    back = from_behind(dprev, "outer", -1)
    dkv = spread(down, back)
    return (
        unpack_q(outer_count, seg, dq_low, dq_high),
        *unpack_kv(outer_count, seg, dkv),
    )


def solution(mesh):
    spec = P(("inner", "outer"), None)
    return jax.shard_map(
        local,
        mesh=mesh,
        in_specs=(spec, spec, spec, spec, P()),
        out_specs=(spec, spec, spec),
        check_vma=False,
    )
```
